256 devices in a mesh: ctx: 64 (over y, z, core), tp: 4 (over x).
Axes of the slice: x: 4, y: 4, z: 8, core: 2. Of those that a mesh axis runs over, the one named last changes fastest.
Arguments:
- gate_branch: bfloat16 [8192, 4096], P('ctx', 'tp'), may hold values from -520 to 520
- key_branch: bfloat16 [8192, 4096], P('ctx', 'tp'), may hold values from -6 to 6
- value_branch: bfloat16 [8192, 4096], P('ctx', 'tp'), may hold values from -6 to 6
- spectrum_real: float32 [128, 128, 4096], P(None, 'ctx', 'tp'), may hold values from -6 to 6
- spectrum_imag: float32 [128, 128, 4096], P(None, 'ctx', 'tp'), may hold values from -6 to 6
- norm_gain: float32 [4096], P('tp'), may hold values from 0.1 to 1.9
Outputs:
- mixed: bfloat16 [8192, 4096], P('ctx', 'tp')
The draws below stay inside these ranges and needn't reach their ends.
All inputs are finite; a program needn't handle non-finite values.
Results may differ from the reference program's by a relative error of at most 0.001.
Values sent between devices are 32-bit elements; how exact they have to be, the bound alone decides.
A program may use at most 64 MiB of HBM per device.

```python
import math
import jax
import jax.numpy as jnp
import numpy as np
from jax import lax

CH = 4096
TOK_DEV = 128
TOKENS = 8192
FFT_LEN = 16384
N_CTX = 64


def draw_gate_branch(key, part):
    key_base = jax.random.fold_in(key, 11)
    key_rows = jax.random.fold_in(key, 12)
    column = jnp.arange(CH, dtype=jnp.float32) / max(CH - 1, 1)
    base_draw = jnp.clip(jax.random.normal(key_base, (TOKENS, CH), jnp.float32), -4.0, 4.0)
    channel_ramp = jnp.exp(math.log(10.0) * column)
    row_scale = jnp.exp(math.log(10.0) * jax.random.uniform(key_rows, (TOKENS, 1), jnp.float32))
    return (base_draw * channel_ramp[None, :] * row_scale).astype(jnp.bfloat16)


def steps_of(rng, shape, pieces, least, high):
    def one(position, blocks):
        heights = jax.random.uniform(jax.random.fold_in(jax.random.fold_in(rng, 6), position), (blocks,), jnp.float32, least / len(pieces), high / len(pieces))
        return jnp.repeat(jnp.exp(heights), shape[position] // blocks).reshape((-1,) + (1,) * (len(shape) - position - 1))

    loudness = one(*pieces[0])
    for cut in pieces[1:]:
        loudness = loudness * one(*cut)
    return loudness


def noise(rng, extent, deviation, most, shards=(), kind=jnp.bfloat16):
    drawn = deviation * jax.random.normal(rng, extent, jnp.float32)
    if shards:
        drawn = drawn * steps_of(rng, extent, shards, -0.22, 0.18)
    return jnp.clip(drawn, -most, most).astype(kind)


def setup_inputs(seed: int = 0) -> dict:
    key_of = jax.random.split(jax.random.key(seed), 7)
    return {
        "gate_branch": draw_gate_branch(jax.random.fold_in(key_of[6], 71), 0),
        "key_branch": noise(key_of[1], (TOKENS, CH), 1.0, 6.0, ((0, 64), (1, 4))),
        "value_branch": noise(key_of[2], (TOKENS, CH), 1.0, 6.0, ((0, 64), (1, 4))),
        "spectrum_real": noise(key_of[3], (TOK_DEV, 2 * N_CTX, CH), 1.0, 6.0, ((1, 64), (2, 4)), jnp.float32),
        "spectrum_imag": noise(key_of[4], (TOK_DEV, 2 * N_CTX, CH), 1.0, 6.0, ((1, 64), (2, 4)), jnp.float32),
        "norm_gain": jnp.clip(1.0 + 0.18 * jax.random.normal(key_of[5], (CH,), jnp.float32), 0.1, 1.9),
    }


epsilon = 1e-05

def reversed_bits(values, count_bits):
    result = values * 0
    for bit_level in range(count_bits):
        result = result | (values >> bit_level & 1) << count_bits - 1 - bit_level
    return result

def reference(gate_branch, key_branch, value_branch, spectrum_real, spectrum_imag, norm_gain):
    signal = key_branch.astype(jnp.float32) * value_branch.astype(jnp.float32)
    padded = jnp.concatenate([signal, jnp.zeros_like(signal)], axis=0)
    freq_signal = jnp.fft.fft(padded, axis=0)
    count_bits = N_CTX.bit_length() - 1
    slot_ids = np.arange(2 * N_CTX)
    freq_low = 2 * reversed_bits(slot_ids // 2, count_bits) + slot_ids % 2
    freq_order = (freq_low[None, :] + 2 * N_CTX * np.arange(TOK_DEV)[:, None]).reshape(-1)
    inverse_order = np.argsort(freq_order)
    spectrum = lax.complex(spectrum_real, spectrum_imag).reshape(FFT_LEN, CH)[inverse_order]
    convolved = jnp.real(jnp.fft.ifft(freq_signal * spectrum, axis=0))[:TOKENS]
    gated = gate_branch.astype(jnp.float32) * convolved
    mean_square = lax.optimization_barrier(jnp.mean(gated * gated, axis=1, keepdims=True))
    return (gated * lax.rsqrt(mean_square + epsilon) * norm_gain[None, :]).astype(jnp.bfloat16)
```

```python
import functools

import jax
import jax.numpy as jnp
import ml_dtypes
import numpy as np
from jax import lax
from jax.experimental import pallas as pl
from jax.experimental.pallas import tpu as pltpu
from jax.sharding import PartitionSpec as P

MESH = pl.DeviceIdType.MESH
F32 = jnp.float32
BF16 = jnp.bfloat16
N = 64
TP = 4
TOK = 128
CHAN = 1024
FFT = 2 * N * TOK
EPS = 1e-05
HALF = CHAN // 2
GROUP = 8


def split_table(table):
    high = table.astype(ml_dtypes.bfloat16)
    low = (table - high.astype(np.float64)).astype(ml_dtypes.bfloat16)
    return high, low


def tables():
    bits = N.bit_length() - 1
    place = np.arange(N)
    rev = np.zeros_like(place)
    for bit in range(bits):
        rev |= (place >> bit & 1) << (bits - 1 - bit)
    residue = np.concatenate([2 * rev, 2 * rev + 1])
    block = np.arange(N)
    pos = np.arange(TOK)
    angle = 2 * np.pi / (2 * N) * ((residue[:, None] * block[None, :]) % (2 * N))
    first = np.concatenate([np.cos(angle), -np.sin(angle)])
    high, low = split_table(first)
    first_cat = np.concatenate([high, high, low], axis=1)
    last = np.concatenate([np.cos(angle), -np.sin(angle)]).T / FFT
    high, low = split_table(last)
    last_cat = np.concatenate([high, high, low], axis=1)
    turn = 2 * np.pi / FFT * ((residue[:, None] * pos[None, :]) % FFT)
    inner = 2 * np.pi / TOK * ((pos[:, None] * pos[None, :]) % TOK)
    cos, sin = np.cos(inner), np.sin(inner)
    forward = np.block([[cos, -sin], [sin, cos]])
    high, low = split_table(forward)
    forward_cat = np.concatenate([high, high, low], axis=0)
    backward = np.block([[cos, sin], [-sin, cos]])
    high, low = split_table(backward)
    backward_cat = np.concatenate([high, high, low], axis=0)
    return (
        first_cat,
        forward_cat,
        backward_cat,
        last_cat,
        np.cos(turn).astype(np.float32),
        np.sin(turn).astype(np.float32),
    )


def parts(value):
    high = value.astype(BF16)
    return high, (value - high.astype(F32)).astype(BF16)


def kernel(
    gate_ref,
    key_ref,
    value_ref,
    real_ref,
    imag_ref,
    gain_ref,
    first_ref,
    forward_ref,
    backward_ref,
    last_ref,
    cos_ref,
    sin_ref,
    out_ref,
    sig_send,
    sig_recv,
    fil_send,
    fil_recv,
    freq,
    rows_wide,
    cols_sig,
    cols_wide,
    res_send,
    res_recv,
    gate_t,
    gated,
    sum_send,
    sum_recv,
    send_sem,
    sig_sem,
    fil_sem,
    res_sem,
    sum_sem,
    own_sem,
):
    me = lax.axis_index("ctx")
    tp = lax.axis_index("tp")
    barrier = pltpu.get_barrier_semaphore()

    def greet(k, carry):
        pl.semaphore_signal(
            barrier, inc=1, device_id={"ctx": (me + k) % N}, device_id_type=MESH
        )
        return carry

    lax.fori_loop(1, N, greet, 0)
    for k in range(1, TP):
        pl.semaphore_signal(
            barrier, inc=1, device_id={"tp": (tp + k) % TP}, device_id_type=MESH
        )

    for j in range(8):
        lanes = pl.ds(j * 128, 128)
        signal = key_ref[:, lanes].astype(F32) * value_ref[:, lanes].astype(F32)
        turned = signal.T
        for i in range(16):
            device = (j % 4) * 16 + i
            sig_send[pl.ds(device * 16 + (j // 4) * 8, 8), :] = turned[i * 8 : i * 8 + 8]

    for j in range(8):
        for e in range(2):
            for part, ref in enumerate((real_ref, imag_ref)):
                turned = ref[pl.ds(j * 2 + e, 128, stride=16), :].T
                for i in range(16):
                    device = (j % 4) * 16 + i
                    row = (((j // 4) * N + device) * 4 + e * 2 + part) * 8
                    fil_send[pl.ds(row, 8), :] = turned[i * 8 : i * 8 + 8]

    pl.semaphore_wait(barrier, N - 1 + TP - 1)

    def send_signal(k, carry):
        peer = (me + k) % N
        pltpu.make_async_remote_copy(
            sig_send.at[pl.ds(peer * 16, 16)],
            sig_recv.at[pl.ds(me * 16, 16)],
            send_sem.at[0],
            sig_sem,
            device_id={"ctx": peer},
            device_id_type=MESH,
        ).start()
        return carry

    lax.fori_loop(1, N, send_signal, 0)

    for h in range(2):

        def send_filter(k, carry):
            peer = (me + k) % N
            pltpu.make_async_remote_copy(
                fil_send.at[pl.ds((h * N + peer) * 32, 32)],
                fil_recv.at[pl.ds((h * N + me) * 32, 32)],
                send_sem.at[1 + h],
                fil_sem.at[h],
                device_id={"ctx": peer},
                device_id_type=MESH,
            ).start()
            return carry

        lax.fori_loop(1, N, send_filter, 0)

    own = [
        pltpu.make_async_copy(
            sig_send.at[pl.ds(me * 16, 16)], sig_recv.at[pl.ds(me * 16, 16)], own_sem.at[0]
        )
    ]
    for h in range(2):
        rows = pl.ds((h * N + me) * 32, 32)
        own.append(
            pltpu.make_async_copy(fil_send.at[rows], fil_recv.at[rows], own_sem.at[1 + h])
        )
    for copy in own:
        copy.start()

    for j in range(8):
        gate_t[pl.ds(j * 128, 128), :] = gate_ref[:, pl.ds(j * 128, 128)].astype(F32).T

    def landed(buffer, rows, sem):
        view = buffer.at[pl.ds(0, rows)]
        pltpu.make_async_copy(view, view, sem).wait()

    own[0].wait()
    landed(sig_recv, (N - 1) * 16, sig_sem)

    for h in range(2):
        for c in range(GROUP):
            high, low = parts(sig_recv[pl.ds(h * 8 + c, N, stride=16), :])
            lanes = pl.ds(c * 128, 128)
            cols_sig[pl.ds(0, N), lanes] = high
            cols_sig[pl.ds(N, N), lanes] = low
            cols_sig[pl.ds(2 * N, N), lanes] = high
        for c in range(GROUP):
            lanes = pl.ds(c * 128, 128)
            mid = jnp.dot(first_ref[...], cols_sig[:, lanes], preferred_element_type=F32)
            re, im = mid[:128], mid[128:]
            cos, sin = cos_ref[...], sin_ref[...]
            rows = pl.ds(c * 128, 128)
            high, low = parts(re * cos + im * sin)
            rows_wide[rows, pl.ds(0, 128)] = high
            rows_wide[rows, pl.ds(256, 128)] = low
            rows_wide[rows, pl.ds(512, 128)] = high
            high, low = parts(im * cos - re * sin)
            rows_wide[rows, pl.ds(128, 128)] = high
            rows_wide[rows, pl.ds(384, 128)] = low
            rows_wide[rows, pl.ds(640, 128)] = high
        for c in range(0, GROUP, 2):
            rows = pl.ds(c * 128, 256)
            freq[pl.ds((h * GROUP + c) * 128, 256), :] = jnp.dot(
                rows_wide[rows, :], forward_ref[...], preferred_element_type=F32
            )

    for h in range(2):
        own[1 + h].wait()
        landed(fil_recv, (N - 1) * 32, fil_sem.at[h])
        for c in range(GROUP):
            for e in range(2):
                base = h * N * 32 + e * 16 + c
                f_re = fil_recv[pl.ds(base, N, stride=32), :]
                f_im = fil_recv[pl.ds(base + 8, N, stride=32), :]
                src = pl.ds((h * GROUP + c) * 128 + e * N, N)
                x_re = freq[src, pl.ds(0, 128)]
                x_im = freq[src, pl.ds(128, 128)]
                rows = pl.ds(c * 128 + e * N, N)
                high, low = parts(x_re * f_re - x_im * f_im)
                rows_wide[rows, pl.ds(0, 128)] = high
                rows_wide[rows, pl.ds(256, 128)] = low
                rows_wide[rows, pl.ds(512, 128)] = high
                high, low = parts(x_re * f_im + x_im * f_re)
                rows_wide[rows, pl.ds(128, 128)] = high
                rows_wide[rows, pl.ds(384, 128)] = low
                rows_wide[rows, pl.ds(640, 128)] = high
        for c in range(0, GROUP, 2):
            rows = pl.ds(c * 128, 256)
            back = jnp.dot(rows_wide[rows, :], backward_ref[...], preferred_element_type=F32)
            cos, sin = cos_ref[...], sin_ref[...]
            for i in range(2):
                lanes = pl.ds((c + i) * 128, 128)
                re = back[i * 128 : i * 128 + 128, :128]
                im = back[i * 128 : i * 128 + 128, 128:]
                high, low = parts(re * cos - im * sin)
                cols_wide[pl.ds(0, 128), lanes] = high
                cols_wide[pl.ds(256, 128), lanes] = low
                cols_wide[pl.ds(512, 128), lanes] = high
                high, low = parts(re * sin + im * cos)
                cols_wide[pl.ds(128, 128), lanes] = high
                cols_wide[pl.ds(384, 128), lanes] = low
                cols_wide[pl.ds(640, 128), lanes] = high
        for c in range(0, GROUP, 2):
            conv = jnp.dot(
                last_ref[...], cols_wide[:, pl.ds(c * 128, 256)], preferred_element_type=F32
            )
            for i in range(2):
                res_send[pl.ds(h * HALF + c + i, N, stride=8), :] = conv[:, i * 128 : i * 128 + 128]

        def send_result(k, carry):
            peer = (me + k) % N
            pltpu.make_async_remote_copy(
                res_send.at[pl.ds(h * HALF + peer * 8, 8)],
                res_recv.at[pl.ds(h * HALF + me * 8, 8)],
                send_sem.at[3 + h],
                res_sem.at[h],
                device_id={"ctx": peer},
                device_id_type=MESH,
            ).start()
            return carry

        lax.fori_loop(1, N, send_result, 0)
        rows = pl.ds(h * HALF + me * 8, 8)
        res_recv[rows, :] = res_send[rows, :]

    total = jnp.zeros((8, 128), F32)
    for h in range(2):
        landed(res_recv, (N - 1) * 8, res_sem.at[h])
        for j in range(4):
            rows = pl.ds(h * HALF + j * 128, 128)
            value = res_recv[rows, :] * gate_t[rows, :]
            gate_t[rows, :] = value
            total = total + jnp.sum((value * value).reshape(16, 8, 128), axis=0)
    total = jnp.broadcast_to(jnp.sum(total, axis=0, keepdims=True), (8, 128))
    sum_send[...] = total
    copies = []
    for k in range(1, TP):
        copies.append(
            pltpu.make_async_remote_copy(
                sum_send,
                sum_recv.at[k],
                send_sem.at[4 + k],
                sum_sem.at[k],
                device_id={"tp": (tp + k) % TP},
                device_id_type=MESH,
            )
        )
    for copy in copies:
        copy.start()
    for j in range(8):
        lanes = pl.ds(j * 128, 128)
        gated[:, lanes] = gate_t[pl.ds(j * 128, 128), :].T * gain_ref[:, lanes]
    for k, copy in enumerate(copies):
        copy.wait()
        total = total + sum_recv[k + 1]
    scale = lax.rsqrt(total / (CHAN * TP) + EPS)
    scale = jnp.broadcast_to(scale[:1], (128, 128)).T
    for j in range(8):
        lanes = pl.ds(j * 128, 128)
        out_ref[:, lanes] = (gated[:, lanes] * scale).astype(BF16)

    landed(sig_send, (N - 1) * 16, send_sem.at[0])
    for h in range(2):
        landed(fil_send, (N - 1) * 32, send_sem.at[1 + h])
        landed(res_send, (N - 1) * 8, send_sem.at[3 + h])


def local(gate_branch, key_branch, value_branch, spectrum_real, spectrum_imag, norm_gain):
    def lines(spectrum):
        split = spectrum.reshape(TOK, 2, CHAN // 128, 128)
        return split.transpose(0, 2, 1, 3).reshape(TOK * 2 * CHAN // 128, 128)

    args = (
        gate_branch,
        key_branch,
        value_branch,
        lines(spectrum_real),
        lines(spectrum_imag),
        norm_gain.reshape(1, CHAN),
    ) + tuple(jnp.asarray(table) for table in tables())
    vmem = pl.BlockSpec(memory_space=pltpu.VMEM)
    return pl.pallas_call(
        kernel,
        out_shape=jax.ShapeDtypeStruct((TOK, CHAN), BF16),
        in_specs=[vmem] * len(args),
        out_specs=vmem,
        scratch_shapes=[
            pltpu.VMEM((CHAN, 128), F32),
            pltpu.VMEM((CHAN, 128), F32),
            pltpu.VMEM((4 * CHAN, 128), F32),
            pltpu.VMEM((4 * CHAN, 128), F32),
            pltpu.VMEM((2 * GROUP * 128, 256), F32),
            pltpu.VMEM((GROUP * 128, 768), BF16),
            pltpu.VMEM((3 * N, GROUP * 128), BF16),
            pltpu.VMEM((768, GROUP * 128), BF16),
            pltpu.VMEM((CHAN, 128), F32),
            pltpu.VMEM((CHAN, 128), F32),
            pltpu.VMEM((CHAN, 128), F32),
            pltpu.VMEM((TOK, CHAN), F32),
            pltpu.VMEM((8, 128), F32),
            pltpu.VMEM((TP, 8, 128), F32),
            pltpu.SemaphoreType.DMA((8,)),
            pltpu.SemaphoreType.DMA,
            pltpu.SemaphoreType.DMA((2,)),
            pltpu.SemaphoreType.DMA((2,)),
            pltpu.SemaphoreType.DMA((TP,)),
            pltpu.SemaphoreType.DMA((3,)),
        ],
        compiler_params=pltpu.CompilerParams(
            collective_id=0, has_side_effects=True, vmem_limit_bytes=48 << 20
        ),
    )(*args)


def solution(mesh):
    in_specs = (
        P("ctx", "tp"),
        P("ctx", "tp"),
        P("ctx", "tp"),
        P(None, "ctx", "tp"),
        P(None, "ctx", "tp"),
        P("tp"),
    )
    return jax.shard_map(
        local, mesh=mesh, in_specs=in_specs, out_specs=P("ctx", "tp"), check_vma=False
    )
```

```python
import functools

import jax
import jax.numpy as jnp
import ml_dtypes
import numpy as np
from jax import lax
from jax.experimental import pallas as pl
from jax.experimental.pallas import tpu as pltpu
from jax.sharding import PartitionSpec as P

MESH = pl.DeviceIdType.MESH
F32 = jnp.float32
BF16 = jnp.bfloat16
N = 64
TP = 4
TOK = 128
CHAN = 1024
FFT = 2 * N * TOK
EPS = 1e-05
HALF = CHAN // 2
GROUP = 8


def split_table(table):
    high = table.astype(ml_dtypes.bfloat16)
    low = (table - high.astype(np.float64)).astype(ml_dtypes.bfloat16)
    return high, low


def tables():
    bits = N.bit_length() - 1
    place = np.arange(N)
    rev = np.zeros_like(place)
    for bit in range(bits):
        rev |= (place >> bit & 1) << (bits - 1 - bit)
    residue = np.concatenate([2 * rev, 2 * rev + 1])
    block = np.arange(N)
    pos = np.arange(TOK)
    angle = 2 * np.pi / (2 * N) * ((residue[:, None] * block[None, :]) % (2 * N))
    first = np.concatenate([np.cos(angle), -np.sin(angle)])
    high, low = split_table(first)
    first_cat = np.concatenate([high, high, low], axis=1)
    last = np.concatenate([np.cos(angle), -np.sin(angle)]).T / FFT
    high, low = split_table(last)
    last_cat = np.concatenate([high, high, low], axis=1)
    turn = 2 * np.pi / FFT * ((residue[:, None] * pos[None, :]) % FFT)
    inner = 2 * np.pi / TOK * ((pos[:, None] * pos[None, :]) % TOK)
    cos, sin = np.cos(inner), np.sin(inner)
    forward = np.block([[cos, -sin], [sin, cos]])
    high, low = split_table(forward)
    forward_cat = np.concatenate([high, high, low], axis=0)
    backward = np.block([[cos, sin], [-sin, cos]])
    high, low = split_table(backward)
    backward_cat = np.concatenate([high, high, low], axis=0)
    return (
        first_cat,
        forward_cat,
        backward_cat,
        last_cat,
        np.cos(turn).astype(np.float32),
        np.sin(turn).astype(np.float32),
    )


def parts(value):
    high = value.astype(BF16)
    return high, (value - high.astype(F32)).astype(BF16)


def kernel(
    gate_hbm,
    key_hbm,
    value_hbm,
    real_hbm,
    imag_hbm,
    gain_hbm,
    first_hbm,
    forward_hbm,
    backward_hbm,
    last_hbm,
    cos_hbm,
    sin_hbm,
    out_ref,
    gate_ref,
    key_ref,
    value_ref,
    real_ref,
    imag_ref,
    gain_ref,
    first_ref,
    forward_ref,
    backward_ref,
    last_ref,
    cos_ref,
    sin_ref,
    sig_send,
    sig_recv,
    fil_send,
    fil_recv,
    freq,
    rows_wide,
    cols_sig,
    cols_wide,
    res_send,
    res_recv,
    gate_t,
    gated,
    sum_send,
    sum_recv,
    send_sem,
    sig_sem,
    fil_sem,
    res_sem,
    sum_sem,
    own_sem,
    load_sem,
):
    pairs = (
        (key_hbm, key_ref),
        (value_hbm, value_ref),
        (real_hbm, real_ref),
        (imag_hbm, imag_ref),
        (first_hbm, first_ref),
        (cos_hbm, cos_ref),
        (sin_hbm, sin_ref),
        (forward_hbm, forward_ref),
        (gate_hbm, gate_ref),
        (backward_hbm, backward_ref),
        (last_hbm, last_ref),
        (gain_hbm, gain_ref),
    )
    loads = [
        pltpu.make_async_copy(src, dst, load_sem.at[i]) for i, (src, dst) in enumerate(pairs)
    ]
    for load in loads:
        load.start()
    me = lax.axis_index("ctx")
    tp = lax.axis_index("tp")
    barrier = pltpu.get_barrier_semaphore()

    def greet(k, carry):
        pl.semaphore_signal(
            barrier, inc=1, device_id={"ctx": (me + k) % N}, device_id_type=MESH
        )
        return carry

    lax.fori_loop(1, N, greet, 0)
    for k in range(1, TP):
        pl.semaphore_signal(
            barrier, inc=1, device_id={"tp": (tp + k) % TP}, device_id_type=MESH
        )

    loads[0].wait()
    loads[1].wait()
    for j in range(8):
        lanes = pl.ds(j * 128, 128)
        signal = key_ref[:, lanes].astype(F32) * value_ref[:, lanes].astype(F32)
        turned = signal.T
        for i in range(16):
            device = (j % 4) * 16 + i
            sig_send[pl.ds(device * 16 + (j // 4) * 8, 8), :] = turned[i * 8 : i * 8 + 8]

    loads[2].wait()
    loads[3].wait()
    for j in range(8):
        for e in range(2):
            for part, ref in enumerate((real_ref, imag_ref)):
                turned = ref[pl.ds(j * 2 + e, 128, stride=16), :].T
                for i in range(16):
                    device = (j % 4) * 16 + i
                    row = (((j // 4) * N + device) * 4 + e * 2 + part) * 8
                    fil_send[pl.ds(row, 8), :] = turned[i * 8 : i * 8 + 8]

    pl.semaphore_wait(barrier, N - 1 + TP - 1)

    def send_signal(k, carry):
        peer = (me + k) % N
        pltpu.make_async_remote_copy(
            sig_send.at[pl.ds(peer * 16, 16)],
            sig_recv.at[pl.ds(me * 16, 16)],
            send_sem.at[0],
            sig_sem,
            device_id={"ctx": peer},
            device_id_type=MESH,
        ).start()
        return carry

    lax.fori_loop(1, N, send_signal, 0)

    for h in range(2):

        def send_filter(k, carry):
            peer = (me + k) % N
            pltpu.make_async_remote_copy(
                fil_send.at[pl.ds((h * N + peer) * 32, 32)],
                fil_recv.at[pl.ds((h * N + me) * 32, 32)],
                send_sem.at[1 + h],
                fil_sem.at[h],
                device_id={"ctx": peer},
                device_id_type=MESH,
            ).start()
            return carry

        lax.fori_loop(1, N, send_filter, 0)

    own = [
        pltpu.make_async_copy(
            sig_send.at[pl.ds(me * 16, 16)], sig_recv.at[pl.ds(me * 16, 16)], own_sem.at[0]
        )
    ]
    for h in range(2):
        rows = pl.ds((h * N + me) * 32, 32)
        own.append(
            pltpu.make_async_copy(fil_send.at[rows], fil_recv.at[rows], own_sem.at[1 + h])
        )
    for copy in own:
        copy.start()

    for load in loads[4:]:
        load.wait()
    for j in range(8):
        gate_t[pl.ds(j * 128, 128), :] = gate_ref[:, pl.ds(j * 128, 128)].astype(F32).T

    def landed(buffer, rows, sem):
        view = buffer.at[pl.ds(0, rows)]
        pltpu.make_async_copy(view, view, sem).wait()

    own[0].wait()
    landed(sig_recv, (N - 1) * 16, sig_sem)

    for h in range(2):
        for c in range(GROUP):
            high, low = parts(sig_recv[pl.ds(h * 8 + c, N, stride=16), :])
            lanes = pl.ds(c * 128, 128)
            cols_sig[pl.ds(0, N), lanes] = high
            cols_sig[pl.ds(N, N), lanes] = low
            cols_sig[pl.ds(2 * N, N), lanes] = high
        for c in range(GROUP):
            lanes = pl.ds(c * 128, 128)
            mid = jnp.dot(first_ref[...], cols_sig[:, lanes], preferred_element_type=F32)
            re, im = mid[:128], mid[128:]
            cos, sin = cos_ref[...], sin_ref[...]
            rows = pl.ds(c * 128, 128)
            high, low = parts(re * cos + im * sin)
            rows_wide[rows, pl.ds(0, 128)] = high
            rows_wide[rows, pl.ds(256, 128)] = low
            rows_wide[rows, pl.ds(512, 128)] = high
            high, low = parts(im * cos - re * sin)
            rows_wide[rows, pl.ds(128, 128)] = high
            rows_wide[rows, pl.ds(384, 128)] = low
            rows_wide[rows, pl.ds(640, 128)] = high
        for c in range(0, GROUP, 2):
            rows = pl.ds(c * 128, 256)
            freq[pl.ds((h * GROUP + c) * 128, 256), :] = jnp.dot(
                rows_wide[rows, :], forward_ref[...], preferred_element_type=F32
            )

    for h in range(2):
        own[1 + h].wait()
        landed(fil_recv, (N - 1) * 32, fil_sem.at[h])
        for c in range(GROUP):
            for e in range(2):
                base = h * N * 32 + e * 16 + c
                f_re = fil_recv[pl.ds(base, N, stride=32), :]
                f_im = fil_recv[pl.ds(base + 8, N, stride=32), :]
                src = pl.ds((h * GROUP + c) * 128 + e * N, N)
                x_re = freq[src, pl.ds(0, 128)]
                x_im = freq[src, pl.ds(128, 128)]
                rows = pl.ds(c * 128 + e * N, N)
                high, low = parts(x_re * f_re - x_im * f_im)
                rows_wide[rows, pl.ds(0, 128)] = high
                rows_wide[rows, pl.ds(256, 128)] = low
                rows_wide[rows, pl.ds(512, 128)] = high
                high, low = parts(x_re * f_im + x_im * f_re)
                rows_wide[rows, pl.ds(128, 128)] = high
                rows_wide[rows, pl.ds(384, 128)] = low
                rows_wide[rows, pl.ds(640, 128)] = high
        for c in range(0, GROUP, 2):
            rows = pl.ds(c * 128, 256)
            back = jnp.dot(rows_wide[rows, :], backward_ref[...], preferred_element_type=F32)
            cos, sin = cos_ref[...], sin_ref[...]
            for i in range(2):
                lanes = pl.ds((c + i) * 128, 128)
                re = back[i * 128 : i * 128 + 128, :128]
                im = back[i * 128 : i * 128 + 128, 128:]
                high, low = parts(re * cos - im * sin)
                cols_wide[pl.ds(0, 128), lanes] = high
                cols_wide[pl.ds(256, 128), lanes] = low
                cols_wide[pl.ds(512, 128), lanes] = high
                high, low = parts(re * sin + im * cos)
                cols_wide[pl.ds(128, 128), lanes] = high
                cols_wide[pl.ds(384, 128), lanes] = low
                cols_wide[pl.ds(640, 128), lanes] = high
        for c in range(0, GROUP, 2):
            conv = jnp.dot(
                last_ref[...], cols_wide[:, pl.ds(c * 128, 256)], preferred_element_type=F32
            )
            for i in range(2):
                res_send[pl.ds(h * HALF + c + i, N, stride=8), :] = conv[:, i * 128 : i * 128 + 128]

        def send_result(k, carry):
            peer = (me + k) % N
            pltpu.make_async_remote_copy(
                res_send.at[pl.ds(h * HALF + peer * 8, 8)],
                res_recv.at[pl.ds(h * HALF + me * 8, 8)],
                send_sem.at[3 + h],
                res_sem.at[h],
                device_id={"ctx": peer},
                device_id_type=MESH,
            ).start()
            return carry

        lax.fori_loop(1, N, send_result, 0)
        rows = pl.ds(h * HALF + me * 8, 8)
        res_recv[rows, :] = res_send[rows, :]

    total = jnp.zeros((8, 128), F32)
    for h in range(2):
        landed(res_recv, (N - 1) * 8, res_sem.at[h])
        for j in range(4):
            rows = pl.ds(h * HALF + j * 128, 128)
            value = res_recv[rows, :] * gate_t[rows, :]
            gate_t[rows, :] = value
            total = total + jnp.sum((value * value).reshape(16, 8, 128), axis=0)
    total = jnp.broadcast_to(jnp.sum(total, axis=0, keepdims=True), (8, 128))
    sum_send[...] = total
    copies = []
    for k in range(1, TP):
        copies.append(
            pltpu.make_async_remote_copy(
                sum_send,
                sum_recv.at[k],
                send_sem.at[4 + k],
                sum_sem.at[k],
                device_id={"tp": (tp + k) % TP},
                device_id_type=MESH,
            )
        )
    for copy in copies:
        copy.start()
    for j in range(8):
        lanes = pl.ds(j * 128, 128)
        gated[:, lanes] = gate_t[pl.ds(j * 128, 128), :].T * gain_ref[:, lanes]
    for k, copy in enumerate(copies):
        copy.wait()
        total = total + sum_recv[k + 1]
    scale = lax.rsqrt(total / (CHAN * TP) + EPS)
    scale = jnp.broadcast_to(scale[:1], (128, 128)).T
    for j in range(8):
        lanes = pl.ds(j * 128, 128)
        out_ref[:, lanes] = (gated[:, lanes] * scale).astype(BF16)

    landed(sig_send, (N - 1) * 16, send_sem.at[0])
    for h in range(2):
        landed(fil_send, (N - 1) * 32, send_sem.at[1 + h])
        landed(res_send, (N - 1) * 8, send_sem.at[3 + h])


def local(gate_branch, key_branch, value_branch, spectrum_real, spectrum_imag, norm_gain):
    def lines(spectrum):
        split = spectrum.reshape(TOK, 2, CHAN // 128, 128)
        return split.transpose(0, 2, 1, 3).reshape(TOK * 2 * CHAN // 128, 128)

    args = (
        gate_branch,
        key_branch,
        value_branch,
        lines(spectrum_real),
        lines(spectrum_imag),
        norm_gain.reshape(1, CHAN),
    ) + tuple(jnp.asarray(table) for table in tables())
    vmem = pl.BlockSpec(memory_space=pltpu.VMEM)
    hbm = pl.BlockSpec(memory_space=pltpu.HBM)
    return pl.pallas_call(
        kernel,
        out_shape=jax.ShapeDtypeStruct((TOK, CHAN), BF16),
        in_specs=[hbm] * len(args),
        out_specs=vmem,
        scratch_shapes=[pltpu.VMEM(arg.shape, arg.dtype) for arg in args]
        + [
            pltpu.VMEM((CHAN, 128), F32),
            pltpu.VMEM((CHAN, 128), F32),
            pltpu.VMEM((4 * CHAN, 128), F32),
            pltpu.VMEM((4 * CHAN, 128), F32),
            pltpu.VMEM((2 * GROUP * 128, 256), F32),
            pltpu.VMEM((GROUP * 128, 768), BF16),
            pltpu.VMEM((3 * N, GROUP * 128), BF16),
            pltpu.VMEM((768, GROUP * 128), BF16),
            pltpu.VMEM((CHAN, 128), F32),
            pltpu.VMEM((CHAN, 128), F32),
            pltpu.VMEM((CHAN, 128), F32),
            pltpu.VMEM((TOK, CHAN), F32),
            pltpu.VMEM((8, 128), F32),
            pltpu.VMEM((TP, 8, 128), F32),
            pltpu.SemaphoreType.DMA((8,)),
            pltpu.SemaphoreType.DMA,
            pltpu.SemaphoreType.DMA((2,)),
            pltpu.SemaphoreType.DMA((2,)),
            pltpu.SemaphoreType.DMA((TP,)),
            pltpu.SemaphoreType.DMA((3,)),
            pltpu.SemaphoreType.DMA((len(args),)),
        ],
        compiler_params=pltpu.CompilerParams(
            collective_id=0, has_side_effects=True, vmem_limit_bytes=62 << 20
        ),
    )(*args)


def solution(mesh):
    in_specs = (
        P("ctx", "tp"),
        P("ctx", "tp"),
        P("ctx", "tp"),
        P(None, "ctx", "tp"),
        P(None, "ctx", "tp"),
        P("tp"),
    )
    return jax.shard_map(
        local, mesh=mesh, in_specs=in_specs, out_specs=P("ctx", "tp"), check_vma=False
    )
```

```python
import functools

import jax
import jax.numpy as jnp
import ml_dtypes
import numpy as np
from jax import lax
from jax.experimental import pallas as pl
from jax.experimental.pallas import tpu as pltpu
from jax.sharding import PartitionSpec as P

MESH = pl.DeviceIdType.MESH
F32 = jnp.float32
BF16 = jnp.bfloat16
N = 64
TP = 4
TOK = 128
CHAN = 1024
FFT = 2 * N * TOK
EPS = 1e-05
NY, NZ = 4, 8
NEAR = N // 2
SET = CHAN // N
GC = 4
GROUPS = SET // GC
MORE = 4
AHEAD = 2
LAG = 2


def split_table(table):
    high = table.astype(ml_dtypes.bfloat16)
    low = (table - high.astype(np.float64)).astype(ml_dtypes.bfloat16)
    return high, low


def tables():
    bits = N.bit_length() - 1
    place = np.arange(N)
    rev = np.zeros_like(place)
    for bit in range(bits):
        rev |= (place >> bit & 1) << (bits - 1 - bit)
    pos = np.arange(TOK)
    step, y, core = np.meshgrid(np.arange(4), np.arange(NY), np.arange(2), indexing="ij")

    def devices(plane):
        return ((y * NZ + plane % NZ) * 2 + core).reshape(-1)

    first, last, cos_turn, sin_turn = [], [], [], []
    for z in range(NZ):
        for near, far in (
            (devices(z - step), devices(z + 1 + step)),
            (devices(z + step), devices(z - 1 - step)),
        ):
            block = np.concatenate([near, far])
            residue = np.concatenate([2 * rev[near], 2 * rev[near] + 1])
            angle = 2 * np.pi / (2 * N) * ((residue[:, None] * block[None, :]) % (2 * N))
            table = np.concatenate([np.cos(angle), -np.sin(angle)])
            high, low = split_table(table)
            first.append(np.concatenate([high, high, low], axis=1))
            high, low = split_table(table.T / FFT)
            last.append(np.concatenate([high, high, low], axis=1))
            turn = 2 * np.pi / FFT * ((residue[:, None] * pos[None, :]) % FFT)
            cos_turn.append(np.cos(turn).astype(np.float32))
            sin_turn.append(np.sin(turn).astype(np.float32))

    def by_plane(pieces):
        return np.stack(pieces).reshape(NZ, -1, pieces[0].shape[1])

    inner = 2 * np.pi / TOK * ((pos[:, None] * pos[None, :]) % TOK)
    cos, sin = np.cos(inner), np.sin(inner)
    forward = np.block([[cos, -sin], [sin, cos]])
    high, low = split_table(forward)
    forward_cat = np.concatenate([high, high, low], axis=0)
    backward = np.block([[cos, sin], [-sin, cos]])
    high, low = split_table(backward)
    backward_cat = np.concatenate([high, high, low], axis=0)
    return (
        by_plane(first),
        forward_cat,
        backward_cat,
        by_plane(last),
        by_plane(cos_turn),
        by_plane(sin_turn),
    )


def parts(value):
    high = value.astype(BF16)
    return high, (value - high.astype(F32)).astype(BF16)


def device(y, z, core):
    return ((y + NY) % NY * NZ + (z + NZ) % NZ) * 2 + core % 2


def kernel(
    gate_hbm,
    key_hbm,
    value_hbm,
    real_hbm,
    imag_hbm,
    gain_hbm,
    first_hbm,
    forward_hbm,
    backward_hbm,
    last_hbm,
    cos_hbm,
    sin_hbm,
    out_ref,
    gate_ref,
    key_ref,
    value_ref,
    real_ref,
    imag_ref,
    gain_ref,
    first_ref,
    forward_ref,
    backward_ref,
    last_ref,
    cos_ref,
    sin_ref,
    sig_send,
    sig_recv,
    fil_send,
    fil_recv,
    freq,
    rows_wide,
    cols_sig,
    cols_wide,
    far_send,
    far_recv,
    res_send,
    res_recv,
    gate_t,
    gated,
    sum_send,
    sum_recv,
    sig_send_sem,
    sig_recv_sem,
    pass_send_sem,
    pass_recv_sem,
    fil_send_sem,
    fil_recv_sem,
    far_send_sem,
    far_recv_sem,
    res_send_sem,
    res_recv_sem,
    sum_send_sem,
    sum_recv_sem,
    own_sem,
    load_sem,
):
    me = lax.axis_index("ctx")
    tp = lax.axis_index("tp")
    y, z, core = me // (2 * NZ), me // 2 % NZ, me % 2
    up, down = device(y, z + 1, core), device(y, z - 1, core)
    barrier = pltpu.get_barrier_semaphore()

    pairs = (
        (key_hbm, key_ref),
        (value_hbm, value_ref),
        (real_hbm, real_ref),
        (imag_hbm, imag_ref),
        (first_hbm.at[z], first_ref),
        (cos_hbm.at[z], cos_ref),
        (sin_hbm.at[z], sin_ref),
        (forward_hbm, forward_ref),
        (gate_hbm, gate_ref),
        (backward_hbm, backward_ref),
        (last_hbm.at[z], last_ref),
        (gain_hbm, gain_ref),
    )
    loads = [
        pltpu.make_async_copy(src, dst, load_sem.at[i]) for i, (src, dst) in enumerate(pairs)
    ]
    for load in loads:
        load.start()

    def greet(k, carry):
        step = k % 7
        step = (step + 1) // 2 * (2 * (step % 2) - 1)
        peer = device(y + k // 7 % NY, z + step, core + k // 28)
        pl.semaphore_signal(barrier, inc=1, device_id={"ctx": peer}, device_id_type=MESH)
        return carry

    lax.fori_loop(1, 56, greet, 0)
    for k in range(1, TP):
        pl.semaphore_signal(
            barrier, inc=1, device_id={"tp": (tp + k) % TP}, device_id_type=MESH
        )

    loads[0].wait()
    loads[1].wait()
    for j in range(8):
        lanes = pl.ds(j * 128, 128)
        turned = (key_ref[:, lanes].astype(F32) * value_ref[:, lanes].astype(F32)).T
        for i in range(128 // GC):
            group, chan_set = divmod((j * 128) // GC + i, N)
            sig_send[pl.ds(chan_set * SET + group * GC, GC), :] = turned[i * GC : i * GC + GC]

    loads[2].wait()
    loads[3].wait()
    for j in range(8):
        for e in range(2):
            for part, ref in enumerate((real_ref, imag_ref)):
                turned = ref[pl.ds(j * 2 + e, 128, stride=16), :].T
                for i in range(128 // GC):
                    row = (((j * 128) // GC + i) * 4 + e * 2 + part) * GC
                    fil_send[pl.ds(row, GC), :] = turned[i * GC : i * GC + GC]

    pl.semaphore_wait(barrier, 55 + TP - 1)

    def reach(m):
        step = m % 4
        return y + m // 4 % NY, core + m // 16, step, step * 8 + y * 2 + core

    def send_signal(m, carry):
        to_y, to_core, step, slot = reach(m)
        for side in range(2):
            plane = z + step if side == 0 else z - step
            chan_set = device(to_y, plane - side, to_core)
            pltpu.make_async_remote_copy(
                sig_send.at[pl.ds(chan_set * SET, SET)],
                sig_recv.at[pl.ds((side * N + slot) * SET, SET)],
                sig_send_sem,
                sig_recv_sem,
                device_id={"ctx": device(to_y, plane, to_core)},
                device_id_type=MESH,
            ).start()
        return carry

    lax.fori_loop(1, NEAR, send_signal, 0)

    def send_filter(group):
        def send(m, carry):
            to_y, to_core, step, slot = reach(m)
            for side in range(2):
                plane = z + step if side == 0 else z - step
                chan_set = device(to_y, plane - side, to_core)
                pltpu.make_async_remote_copy(
                    fil_send.at[pl.ds((group * N + chan_set) * 4 * GC, 4 * GC)],
                    fil_recv.at[pl.ds(((group * 2 + side) * NEAR + slot) * 4 * GC, 4 * GC)],
                    fil_send_sem.at[group],
                    fil_recv_sem.at[group],
                    device_id={"ctx": device(to_y, plane, to_core)},
                    device_id_type=MESH,
                ).start()
            return carry

        lax.fori_loop(1, NEAR, send, 0)

    for group in range(AHEAD):
        send_filter(group)

    sets = (me, down)
    own_slot = y * 2 + core
    own_signal, own_filter = [], []
    for side in range(2):
        own_signal.append(
            pltpu.make_async_copy(
                sig_send.at[pl.ds(sets[side] * SET, SET)],
                sig_recv.at[pl.ds((side * N + own_slot) * SET, SET)],
                own_sem.at[side],
            )
        )
        for group in range(GROUPS):
            own_filter.append(
                pltpu.make_async_copy(
                    fil_send.at[pl.ds((group * N + sets[side]) * 4 * GC, 4 * GC)],
                    fil_recv.at[pl.ds(((group * 2 + side) * NEAR + own_slot) * 4 * GC, 4 * GC)],
                    own_sem.at[2 + side * GROUPS + group],
                )
            )
    for copy in own_signal + own_filter:
        copy.start()

    for load in loads[4:]:
        load.wait()
    for j in range(8):
        gate_t[pl.ds(j * 128, 128), :] = gate_ref[:, pl.ds(j * 128, 128)].astype(F32).T

    def landed(buffer, rows, sem):
        view = buffer.at[pl.ds(0, rows)]
        pltpu.make_async_copy(view, view, sem).wait()

    for copy in own_signal:
        copy.wait()
    landed(sig_recv, 2 * (NEAR - 1) * SET, sig_recv_sem)
    passes = [
        pltpu.make_async_remote_copy(
            sig_recv.at[pl.ds(side * N * SET, NEAR * SET)],
            sig_recv.at[pl.ds(((1 - side) * N + NEAR) * SET, NEAR * SET)],
            pass_send_sem.at[side],
            pass_recv_sem.at[1 - side],
            device_id={"ctx": (up, down)[side]},
            device_id_type=MESH,
        )
        for side in range(2)
    ]
    for copy in passes:
        copy.start()
    for group in range(AHEAD, MORE):
        send_filter(group)
    for side in range(2):
        far = sig_recv.at[pl.ds((side * N + NEAR) * SET, NEAR * SET)]
        pltpu.make_async_copy(far, far, pass_recv_sem.at[side]).wait()

    for side in range(2):
        for c in range(SET):
            high, low = parts(sig_recv[pl.ds(side * N * SET + c, N, stride=SET), :])
            lanes = pl.ds(c * 128, 128)
            cols_sig[pl.ds(0, N), lanes] = high
            cols_sig[pl.ds(N, N), lanes] = low
            cols_sig[pl.ds(2 * N, N), lanes] = high
        cos, sin = cos_ref[pl.ds(side * N, N), :], sin_ref[pl.ds(side * N, N), :]
        for pair in range(SET // 2):
            mid = jnp.dot(
                first_ref[pl.ds(side * 128, 128), :],
                cols_sig[:, pl.ds(pair * 256, 256)],
                preferred_element_type=F32,
            )
            for i in range(2):
                re, im = mid[:N, i * 128 : i * 128 + 128], mid[N:, i * 128 : i * 128 + 128]
                rows = pl.ds((pair * 2 + i) * N, N)
                high, low = parts(re * cos + im * sin)
                rows_wide[rows, pl.ds(0, 128)] = high
                rows_wide[rows, pl.ds(256, 128)] = low
                rows_wide[rows, pl.ds(512, 128)] = high
                high, low = parts(im * cos - re * sin)
                rows_wide[rows, pl.ds(128, 128)] = high
                rows_wide[rows, pl.ds(384, 128)] = low
                rows_wide[rows, pl.ds(640, 128)] = high
        for quad in range(SET // 4):
            freq[pl.ds((side * SET + quad * 4) * N, 4 * N), :] = jnp.dot(
                rows_wide[pl.ds(quad * 4 * N, 4 * N), :],
                forward_ref[...],
                preferred_element_type=F32,
            )

    far_rows = NEAR * GC

    def inverse(group):
        for side in range(2):
            own_filter[side * GROUPS + group].wait()
        landed(fil_recv, 2 * (NEAR - 1) * 4 * GC, fil_recv_sem.at[group])
        for side in range(2):
            for c in range(GC):
                for e in range(2):
                    base = (group * 2 + side) * NEAR * 4 * GC + e * 2 * GC + c
                    f_re = fil_recv[pl.ds(base, NEAR, stride=4 * GC), :]
                    f_im = fil_recv[pl.ds(base + GC, NEAR, stride=4 * GC), :]
                    src = pl.ds((side * SET + group * GC + c) * N + e * NEAR, NEAR)
                    x_re = freq[src, pl.ds(0, 128)]
                    x_im = freq[src, pl.ds(128, 128)]
                    rows = pl.ds((side * GC + c) * N + e * NEAR, NEAR)
                    high, low = parts(x_re * f_re - x_im * f_im)
                    rows_wide[rows, pl.ds(0, 128)] = high
                    rows_wide[rows, pl.ds(256, 128)] = low
                    rows_wide[rows, pl.ds(512, 128)] = high
                    high, low = parts(x_re * f_im + x_im * f_re)
                    rows_wide[rows, pl.ds(128, 128)] = high
                    rows_wide[rows, pl.ds(384, 128)] = low
                    rows_wide[rows, pl.ds(640, 128)] = high
        for quad in range(2 * GC // 4):
            back = jnp.dot(
                rows_wide[pl.ds(quad * 4 * N, 4 * N), :],
                backward_ref[...],
                preferred_element_type=F32,
            )
            for i in range(4):
                side, c = divmod(quad * 4 + i, GC)
                lanes = pl.ds((side * GC + c) * 128, 128)
                cos, sin = cos_ref[pl.ds(side * N, N), :], sin_ref[pl.ds(side * N, N), :]
                re, im = back[i * N : i * N + N, :128], back[i * N : i * N + N, 128:]
                high, low = parts(re * cos - im * sin)
                cols_wide[pl.ds(0, N), lanes] = high
                cols_wide[pl.ds(2 * N, N), lanes] = low
                cols_wide[pl.ds(4 * N, N), lanes] = high
                high, low = parts(re * sin + im * cos)
                cols_wide[pl.ds(N, N), lanes] = high
                cols_wide[pl.ds(3 * N, N), lanes] = low
                cols_wide[pl.ds(5 * N, N), lanes] = high
        for side in range(2):
            for pair in range(GC // 2):
                conv = jnp.dot(
                    last_ref[pl.ds(side * N, N), :],
                    cols_wide[:, pl.ds((side * GC + pair * 2) * 128, 256)],
                    preferred_element_type=F32,
                )
                for i in range(2):
                    base = (group * 2 + side) * far_rows + pair * 2 + i
                    rows = pl.ds(base, NEAR, stride=GC)
                    res_send[rows, :] = conv[:NEAR, i * 128 : i * 128 + 128]
                    far_send[rows, :] = conv[NEAR:, i * 128 : i * 128 + 128]

    def far_copies(group):
        return [
            pltpu.make_async_remote_copy(
                far_send.at[pl.ds((group * 2 + side) * far_rows, far_rows)],
                far_recv.at[pl.ds((group * 2 + 1 - side) * far_rows, far_rows)],
                far_send_sem.at[group * 2 + side],
                far_recv_sem.at[group * 2 + 1 - side],
                device_id={"ctx": (up, down)[side]},
                device_id_type=MESH,
            )
            for side in range(2)
        ]

    own_result = []

    def finish(group):
        for side in range(2):
            rows = pl.ds((group * 2 + side) * far_rows, far_rows)
            view = far_recv.at[rows]
            pltpu.make_async_copy(view, view, far_recv_sem.at[group * 2 + side]).wait()
            res_send[rows, :] = res_send[rows, :] + far_recv[rows, :]

        def send(m, carry):
            step = m % 4
            to_y, to_core = (y + m // 4) % NY, (core + m // 16) % 2
            slot = step * 8 + to_y * 2 + to_core
            for side in range(2):
                plane = z - step if side == 0 else z + step
                pltpu.make_async_remote_copy(
                    res_send.at[pl.ds(((group * 2 + side) * NEAR + slot) * GC, GC)],
                    res_recv.at[pl.ds((group * N + sets[side]) * GC, GC)],
                    res_send_sem.at[group],
                    res_recv_sem.at[group],
                    device_id={"ctx": device(to_y, plane, to_core)},
                    device_id_type=MESH,
                ).start()
            return carry

        lax.fori_loop(1, NEAR, send, 0)
        for side in range(2):
            copy = pltpu.make_async_copy(
                res_send.at[pl.ds(((group * 2 + side) * NEAR + own_slot) * GC, GC)],
                res_recv.at[pl.ds((group * N + sets[side]) * GC, GC)],
                own_sem.at[side],
            )
            copy.start()
            own_result.append(copy)

    for group in range(GROUPS):
        inverse(group)
        for copy in far_copies(group):
            copy.start()
        if group + MORE < GROUPS:
            send_filter(group + MORE)
        if group >= LAG:
            finish(group - LAG)
    for group in range(GROUPS - LAG, GROUPS):
        finish(group)

    for side in range(2):
        view = res_send.at[pl.ds(0, GROUPS * GC)]
        pltpu.make_async_copy(view, view, own_sem.at[side]).wait()
    total = jnp.zeros((8, 128), F32)
    for group in range(GROUPS):
        landed(res_recv, 2 * (NEAR - 1) * GC, res_recv_sem.at[group])
        for j in range(N * GC // 128):
            rows = pl.ds(group * N * GC + j * 128, 128)
            value = res_recv[rows, :] * gate_t[rows, :]
            gate_t[rows, :] = value
            total = total + jnp.sum((value * value).reshape(16, 8, 128), axis=0)
    total = jnp.broadcast_to(jnp.sum(total, axis=0, keepdims=True), (8, 128))
    sum_send[...] = total
    copies = []
    for k in range(1, TP):
        copies.append(
            pltpu.make_async_remote_copy(
                sum_send,
                sum_recv.at[k],
                sum_send_sem.at[k],
                sum_recv_sem.at[k],
                device_id={"tp": (tp + k) % TP},
                device_id_type=MESH,
            )
        )
    for copy in copies:
        copy.start()
    for j in range(8):
        lanes = pl.ds(j * 128, 128)
        gated[:, lanes] = gate_t[pl.ds(j * 128, 128), :].T * gain_ref[:, lanes]
    for k, copy in enumerate(copies):
        copy.wait()
        total = total + sum_recv[k + 1]
    scale = lax.rsqrt(total / (CHAN * TP) + EPS)
    scale = jnp.broadcast_to(scale[:1], (128, 128)).T
    for j in range(8):
        lanes = pl.ds(j * 128, 128)
        out_ref[:, lanes] = (gated[:, lanes] * scale).astype(BF16)

    landed(sig_send, 2 * (NEAR - 1) * SET, sig_send_sem)
    for copy in passes:
        copy.wait_send()
    for group in range(GROUPS):
        landed(fil_send, 2 * (NEAR - 1) * 4 * GC, fil_send_sem.at[group])
        for copy in far_copies(group):
            copy.wait_send()
        landed(res_send, 2 * (NEAR - 1) * GC, res_send_sem.at[group])


def local(gate_branch, key_branch, value_branch, spectrum_real, spectrum_imag, norm_gain):
    def lines(spectrum):
        split = spectrum.reshape(TOK, 2, CHAN // 128, 128)
        return split.transpose(0, 2, 1, 3).reshape(TOK * 2 * CHAN // 128, 128)

    args = (
        gate_branch,
        key_branch,
        value_branch,
        lines(spectrum_real),
        lines(spectrum_imag),
        norm_gain.reshape(1, CHAN),
    ) + tuple(jnp.asarray(table) for table in tables())
    vmem = pl.BlockSpec(memory_space=pltpu.VMEM)
    hbm = pl.BlockSpec(memory_space=pltpu.HBM)
    return pl.pallas_call(
        kernel,
        out_shape=jax.ShapeDtypeStruct((TOK, CHAN), BF16),
        in_specs=[hbm] * len(args),
        out_specs=vmem,
        scratch_shapes=[pltpu.VMEM(arg.shape[-2:], arg.dtype) for arg in args]
        + [
            pltpu.VMEM((CHAN, 128), F32),
            pltpu.VMEM((2 * CHAN, 128), F32),
            pltpu.VMEM((4 * CHAN, 128), F32),
            pltpu.VMEM((4 * CHAN, 128), F32),
            pltpu.VMEM((2 * SET * N, 256), F32),
            pltpu.VMEM((SET * N, 768), BF16),
            pltpu.VMEM((3 * N, SET * 128), BF16),
            pltpu.VMEM((6 * N, 2 * GC * 128), BF16),
            pltpu.VMEM((CHAN, 128), F32),
            pltpu.VMEM((CHAN, 128), F32),
            pltpu.VMEM((CHAN, 128), F32),
            pltpu.VMEM((CHAN, 128), F32),
            pltpu.VMEM((CHAN, 128), F32),
            pltpu.VMEM((TOK, CHAN), F32),
            pltpu.VMEM((8, 128), F32),
            pltpu.VMEM((TP, 8, 128), F32),
            pltpu.SemaphoreType.DMA,
            pltpu.SemaphoreType.DMA,
            pltpu.SemaphoreType.DMA((2,)),
            pltpu.SemaphoreType.DMA((2,)),
            pltpu.SemaphoreType.DMA((GROUPS,)),
            pltpu.SemaphoreType.DMA((GROUPS,)),
            pltpu.SemaphoreType.DMA((2 * GROUPS,)),
            pltpu.SemaphoreType.DMA((2 * GROUPS,)),
            pltpu.SemaphoreType.DMA((GROUPS,)),
            pltpu.SemaphoreType.DMA((GROUPS,)),
            pltpu.SemaphoreType.DMA((TP,)),
            pltpu.SemaphoreType.DMA((TP,)),
            pltpu.SemaphoreType.DMA((2 + 2 * GROUPS,)),
            pltpu.SemaphoreType.DMA((len(args),)),
        ],
        compiler_params=pltpu.CompilerParams(
            collective_id=0, has_side_effects=True, vmem_limit_bytes=62 << 20
        ),
    )(*args)


def solution(mesh):
    in_specs = (
        P("ctx", "tp"),
        P("ctx", "tp"),
        P("ctx", "tp"),
        P(None, "ctx", "tp"),
        P(None, "ctx", "tp"),
        P("tp"),
    )
    return jax.shard_map(
        local, mesh=mesh, in_specs=in_specs, out_specs=P("ctx", "tp"), check_vma=False
    )
```

```python
import functools

import jax
import jax.numpy as jnp
import ml_dtypes
import numpy as np
from jax import lax
from jax.experimental import pallas as pl
from jax.experimental.pallas import tpu as pltpu
from jax.sharding import PartitionSpec as P

MESH = pl.DeviceIdType.MESH
F32 = jnp.float32
BF16 = jnp.bfloat16
N = 64
TP = 4
TOK = 128
CHAN = 1024
FFT = 2 * N * TOK
EPS = 1e-05
NY, NZ = 4, 8
NEAR = N // 2
SET = CHAN // N
GC = 4
GROUPS = SET // GC
GROUP_TILES = N * GC // 128
MORE = 4
AHEAD = 2
LAG = 2


def split_table(table):
    high = table.astype(ml_dtypes.bfloat16)
    low = (table - high.astype(np.float64)).astype(ml_dtypes.bfloat16)
    return high, low


def tables():
    bits = N.bit_length() - 1
    place = np.arange(N)
    rev = np.zeros_like(place)
    for bit in range(bits):
        rev |= (place >> bit & 1) << (bits - 1 - bit)
    pos = np.arange(TOK)
    step, y, core = np.meshgrid(np.arange(4), np.arange(NY), np.arange(2), indexing="ij")

    def devices(plane):
        return ((y * NZ + plane % NZ) * 2 + core).reshape(-1)

    first, last, cos_turn, sin_turn = [], [], [], []
    for z in range(NZ):
        for near, far in (
            (devices(z - step), devices(z + 1 + step)),
            (devices(z + step), devices(z - 1 - step)),
        ):
            block = np.concatenate([near, far])
            residue = np.concatenate([2 * rev[near], 2 * rev[near] + 1])
            angle = 2 * np.pi / (2 * N) * ((residue[:, None] * block[None, :]) % (2 * N))
            table = np.concatenate([np.cos(angle), -np.sin(angle)])
            high, low = split_table(table)
            first.append(np.concatenate([high, high, low], axis=1))
            high, low = split_table(table.T / FFT)
            last.append(np.concatenate([high, high, low], axis=1))
            turn = 2 * np.pi / FFT * ((residue[:, None] * pos[None, :]) % FFT)
            cos_turn.append(np.cos(turn).astype(np.float32))
            sin_turn.append(np.sin(turn).astype(np.float32))

    def by_plane(pieces):
        return np.stack(pieces).reshape(NZ, -1, pieces[0].shape[1])

    inner = 2 * np.pi / TOK * ((pos[:, None] * pos[None, :]) % TOK)
    cos, sin = np.cos(inner), np.sin(inner)
    forward = np.block([[cos, -sin], [sin, cos]])
    high, low = split_table(forward)
    forward_cat = np.concatenate([high, high, low], axis=0)
    backward = np.block([[cos, sin], [-sin, cos]])
    high, low = split_table(backward)
    backward_cat = np.concatenate([high, high, low], axis=0)
    return (
        by_plane(first),
        forward_cat,
        backward_cat,
        by_plane(last),
        by_plane(cos_turn),
        by_plane(sin_turn),
    )


def parts(value):
    high = value.astype(BF16)
    return high, (value - high.astype(F32)).astype(BF16)


def device(y, z, core):
    return (y % NY * NZ + (z + NZ) % NZ) * 2 + core % 2


def kernel(
    gate_hbm,
    key_hbm,
    value_hbm,
    real_hbm,
    imag_hbm,
    gain_hbm,
    first_hbm,
    forward_hbm,
    backward_hbm,
    last_hbm,
    cos_hbm,
    sin_hbm,
    out_ref,
    gate_ref,
    key_ref,
    value_ref,
    real_ref,
    imag_ref,
    gain_ref,
    first_ref,
    forward_ref,
    backward_ref,
    last_ref,
    cos_ref,
    sin_ref,
    sig_send,
    sig_recv,
    fil_send,
    fil_recv,
    freq,
    rows_wide,
    cols_sig,
    cols_wide,
    far_send,
    far_recv,
    res_send,
    res_recv,
    gate_t,
    gated,
    sum_send,
    sum_recv,
    sig_send_sem,
    sig_recv_sem,
    pass_send_sem,
    pass_recv_sem,
    fil_send_sem,
    fil_recv_sem,
    far_send_sem,
    far_recv_sem,
    res_send_sem,
    res_recv_sem,
    sum_send_sem,
    sum_recv_sem,
    own_sem,
    load_sem,
):
    me = lax.axis_index("ctx")
    tp = lax.axis_index("tp")
    y, z, core = me // (2 * NZ), me // 2 % NZ, me % 2
    up, down = device(y, z + 1, core), device(y, z - 1, core)
    barrier = pltpu.get_barrier_semaphore()

    def greet(k, carry):
        step = k % 7
        step = (step + 1) // 2 * (2 * (step % 2) - 1)
        peer = device(y + k // 7 % NY, z + step, core + k // 28)
        pl.semaphore_signal(barrier, inc=1, device_id={"ctx": peer}, device_id_type=MESH)
        return carry

    lax.fori_loop(1, 56, greet, 0)
    for k in range(1, TP):
        pl.semaphore_signal(
            barrier, inc=1, device_id={"tp": (tp + k) % TP}, device_id_type=MESH
        )

    pairs = (
        (key_hbm, key_ref),
        (value_hbm, value_ref),
        (real_hbm, real_ref),
        (imag_hbm, imag_ref),
        (first_hbm.at[z], first_ref),
        (cos_hbm.at[z], cos_ref),
        (sin_hbm.at[z], sin_ref),
        (forward_hbm, forward_ref),
        (gate_hbm, gate_ref),
        (backward_hbm, backward_ref),
        (last_hbm.at[z], last_ref),
        (gain_hbm, gain_ref),
    )
    loads = [
        pltpu.make_async_copy(src, dst, load_sem.at[i]) for i, (src, dst) in enumerate(pairs)
    ]
    for load in loads:
        load.start()

    loads[0].wait()
    loads[1].wait()
    for j in range(8):
        lanes = pl.ds(j * 128, 128)
        turned = (key_ref[:, lanes].astype(F32) * value_ref[:, lanes].astype(F32)).T
        for i in range(128 // GC):
            group, chan_set = divmod((j * 128) // GC + i, N)
            sig_send[pl.ds(chan_set * SET + group * GC, GC), :] = turned[i * GC : i * GC + GC]

    pl.semaphore_wait(barrier, 55 + TP - 1)

    def reach(m):
        step = (m % 4 + m // 4) % 4
        return y + m % 4, core + m // 16, step, step * 8 + y * 2 + core

    def send_signal(m, carry):
        to_y, to_core, step, slot = reach(m)
        for side in range(2):
            plane = z + step if side == 0 else z - step
            chan_set = device(to_y, plane - side, to_core)
            pltpu.make_async_remote_copy(
                sig_send.at[pl.ds(chan_set * SET, SET)],
                sig_recv.at[pl.ds((side * N + slot) * SET, SET)],
                sig_send_sem,
                sig_recv_sem,
                device_id={"ctx": device(to_y, plane, to_core)},
                device_id_type=MESH,
            ).start()
        return carry

    lax.fori_loop(1, NEAR, send_signal, 0)

    def turn_filter(group):
        for j in range(group * GROUP_TILES, (group + 1) * GROUP_TILES):
            for e in range(2):
                for part, ref in enumerate((real_ref, imag_ref)):
                    turned = ref[pl.ds(j * 2 + e, 128, stride=16), :].T
                    for i in range(128 // GC):
                        row = (((j * 128) // GC + i) * 4 + e * 2 + part) * GC
                        fil_send[pl.ds(row, GC), :] = turned[i * GC : i * GC + GC]

    def send_filter(group):
        def send(m, carry):
            to_y, to_core, step, slot = reach(m)
            for side in range(2):
                plane = z + step if side == 0 else z - step
                chan_set = device(to_y, plane - side, to_core)
                pltpu.make_async_remote_copy(
                    fil_send.at[pl.ds((group * N + chan_set) * 4 * GC, 4 * GC)],
                    fil_recv.at[pl.ds(((group * 2 + side) * NEAR + slot) * 4 * GC, 4 * GC)],
                    fil_send_sem.at[group],
                    fil_recv_sem.at[group],
                    device_id={"ctx": device(to_y, plane, to_core)},
                    device_id_type=MESH,
                ).start()
            return carry

        lax.fori_loop(1, NEAR, send, 0)

    loads[2].wait()
    loads[3].wait()
    for group in range(GROUPS):
        turn_filter(group)
        if group < AHEAD:
            send_filter(group)

    sets = (me, down)
    own_slot = y * 2 + core
    own_signal, own_filter = [], []
    for side in range(2):
        own_signal.append(
            pltpu.make_async_copy(
                sig_send.at[pl.ds(sets[side] * SET, SET)],
                sig_recv.at[pl.ds((side * N + own_slot) * SET, SET)],
                own_sem.at[side],
            )
        )
        for group in range(GROUPS):
            own_filter.append(
                pltpu.make_async_copy(
                    fil_send.at[pl.ds((group * N + sets[side]) * 4 * GC, 4 * GC)],
                    fil_recv.at[pl.ds(((group * 2 + side) * NEAR + own_slot) * 4 * GC, 4 * GC)],
                    own_sem.at[2 + side * GROUPS + group],
                )
            )
    for copy in own_signal + own_filter:
        copy.start()

    for load in loads[4:]:
        load.wait()
    for j in range(8):
        gate_t[pl.ds(j * 128, 128), :] = gate_ref[:, pl.ds(j * 128, 128)].astype(F32).T

    def landed(buffer, rows, sem):
        view = buffer.at[pl.ds(0, rows)]
        pltpu.make_async_copy(view, view, sem).wait()

    for copy in own_signal:
        copy.wait()
    landed(sig_recv, 2 * (NEAR - 1) * SET, sig_recv_sem)
    passes = [
        pltpu.make_async_remote_copy(
            sig_recv.at[pl.ds(side * N * SET, NEAR * SET)],
            sig_recv.at[pl.ds(((1 - side) * N + NEAR) * SET, NEAR * SET)],
            pass_send_sem.at[side],
            pass_recv_sem.at[1 - side],
            device_id={"ctx": (up, down)[side]},
            device_id_type=MESH,
        )
        for side in range(2)
    ]
    for copy in passes:
        copy.start()
    for group in range(AHEAD, MORE):
        send_filter(group)
    for side in range(2):
        far = sig_recv.at[pl.ds((side * N + NEAR) * SET, NEAR * SET)]
        pltpu.make_async_copy(far, far, pass_recv_sem.at[side]).wait()

    for side in range(2):
        for c in range(SET):
            high, low = parts(sig_recv[pl.ds(side * N * SET + c, N, stride=SET), :])
            lanes = pl.ds(c * 128, 128)
            cols_sig[pl.ds(0, N), lanes] = high
            cols_sig[pl.ds(N, N), lanes] = low
            cols_sig[pl.ds(2 * N, N), lanes] = high
        cos, sin = cos_ref[pl.ds(side * N, N), :], sin_ref[pl.ds(side * N, N), :]
        for pair in range(SET // 2):
            mid = jnp.dot(
                first_ref[pl.ds(side * 128, 128), :],
                cols_sig[:, pl.ds(pair * 256, 256)],
                preferred_element_type=F32,
            )
            for i in range(2):
                re, im = mid[:N, i * 128 : i * 128 + 128], mid[N:, i * 128 : i * 128 + 128]
                rows = pl.ds((pair * 2 + i) * N, N)
                high, low = parts(re * cos + im * sin)
                rows_wide[rows, pl.ds(0, 128)] = high
                rows_wide[rows, pl.ds(256, 128)] = low
                rows_wide[rows, pl.ds(512, 128)] = high
                high, low = parts(im * cos - re * sin)
                rows_wide[rows, pl.ds(128, 128)] = high
                rows_wide[rows, pl.ds(384, 128)] = low
                rows_wide[rows, pl.ds(640, 128)] = high
        for quad in range(SET // 4):
            freq[pl.ds((side * SET + quad * 4) * N, 4 * N), :] = jnp.dot(
                rows_wide[pl.ds(quad * 4 * N, 4 * N), :],
                forward_ref[...],
                preferred_element_type=F32,
            )

    far_rows = NEAR * GC

    def inverse(group):
        for side in range(2):
            own_filter[side * GROUPS + group].wait()
        landed(fil_recv, 2 * (NEAR - 1) * 4 * GC, fil_recv_sem.at[group])
        for side in range(2):
            for c in range(GC):
                for e in range(2):
                    base = (group * 2 + side) * NEAR * 4 * GC + e * 2 * GC + c
                    f_re = fil_recv[pl.ds(base, NEAR, stride=4 * GC), :]
                    f_im = fil_recv[pl.ds(base + GC, NEAR, stride=4 * GC), :]
                    src = pl.ds((side * SET + group * GC + c) * N + e * NEAR, NEAR)
                    x_re = freq[src, pl.ds(0, 128)]
                    x_im = freq[src, pl.ds(128, 128)]
                    rows = pl.ds((side * GC + c) * N + e * NEAR, NEAR)
                    high, low = parts(x_re * f_re - x_im * f_im)
                    rows_wide[rows, pl.ds(0, 128)] = high
                    rows_wide[rows, pl.ds(256, 128)] = low
                    rows_wide[rows, pl.ds(512, 128)] = high
                    high, low = parts(x_re * f_im + x_im * f_re)
                    rows_wide[rows, pl.ds(128, 128)] = high
                    rows_wide[rows, pl.ds(384, 128)] = low
                    rows_wide[rows, pl.ds(640, 128)] = high
        for quad in range(2 * GC // 4):
            back = jnp.dot(
                rows_wide[pl.ds(quad * 4 * N, 4 * N), :],
                backward_ref[...],
                preferred_element_type=F32,
            )
            for i in range(4):
                side, c = divmod(quad * 4 + i, GC)
                lanes = pl.ds((side * GC + c) * 128, 128)
                cos, sin = cos_ref[pl.ds(side * N, N), :], sin_ref[pl.ds(side * N, N), :]
                re, im = back[i * N : i * N + N, :128], back[i * N : i * N + N, 128:]
                high, low = parts(re * cos - im * sin)
                cols_wide[pl.ds(0, N), lanes] = high
                cols_wide[pl.ds(2 * N, N), lanes] = low
                cols_wide[pl.ds(4 * N, N), lanes] = high
                high, low = parts(re * sin + im * cos)
                cols_wide[pl.ds(N, N), lanes] = high
                cols_wide[pl.ds(3 * N, N), lanes] = low
                cols_wide[pl.ds(5 * N, N), lanes] = high
        for side in range(2):
            for pair in range(GC // 2):
                conv = jnp.dot(
                    last_ref[pl.ds(side * N, N), :],
                    cols_wide[:, pl.ds((side * GC + pair * 2) * 128, 256)],
                    preferred_element_type=F32,
                )
                for i in range(2):
                    base = (group * 2 + side) * far_rows + pair * 2 + i
                    rows = pl.ds(base, NEAR, stride=GC)
                    res_send[rows, :] = conv[:NEAR, i * 128 : i * 128 + 128]
                    far_send[rows, :] = conv[NEAR:, i * 128 : i * 128 + 128]

    def far_copies(group):
        return [
            pltpu.make_async_remote_copy(
                far_send.at[pl.ds((group * 2 + side) * far_rows, far_rows)],
                far_recv.at[pl.ds((group * 2 + 1 - side) * far_rows, far_rows)],
                far_send_sem.at[group * 2 + side],
                far_recv_sem.at[group * 2 + 1 - side],
                device_id={"ctx": (up, down)[side]},
                device_id_type=MESH,
            )
            for side in range(2)
        ]

    own_result = []

    def finish(group):
        for side in range(2):
            rows = pl.ds((group * 2 + side) * far_rows, far_rows)
            view = far_recv.at[rows]
            pltpu.make_async_copy(view, view, far_recv_sem.at[group * 2 + side]).wait()
            res_send[rows, :] = res_send[rows, :] + far_recv[rows, :]

        def send(m, carry):
            step = (m % 4 + m // 4) % 4
            to_y, to_core = (y + m % 4) % NY, (core + m // 16) % 2
            slot = step * 8 + to_y * 2 + to_core
            for side in range(2):
                plane = z - step if side == 0 else z + step
                pltpu.make_async_remote_copy(
                    res_send.at[pl.ds(((group * 2 + side) * NEAR + slot) * GC, GC)],
                    res_recv.at[pl.ds((group * N + sets[side]) * GC, GC)],
                    res_send_sem.at[group],
                    res_recv_sem.at[group],
                    device_id={"ctx": device(to_y, plane, to_core)},
                    device_id_type=MESH,
                ).start()
            return carry

        lax.fori_loop(1, NEAR, send, 0, unroll=True)
        for side in range(2):
            copy = pltpu.make_async_copy(
                res_send.at[pl.ds(((group * 2 + side) * NEAR + own_slot) * GC, GC)],
                res_recv.at[pl.ds((group * N + sets[side]) * GC, GC)],
                own_sem.at[side],
            )
            copy.start()
            own_result.append(copy)

    for group in range(GROUPS):
        inverse(group)
        for copy in far_copies(group):
            copy.start()
        if group + MORE < GROUPS:
            send_filter(group + MORE)
        if group >= LAG:
            finish(group - LAG)
    for group in range(GROUPS - LAG, GROUPS):
        finish(group)

    for side in range(2):
        view = res_send.at[pl.ds(0, GROUPS * GC)]
        pltpu.make_async_copy(view, view, own_sem.at[side]).wait()
    total = jnp.zeros((8, 128), F32)
    for group in range(GROUPS):
        landed(res_recv, 2 * (NEAR - 1) * GC, res_recv_sem.at[group])
        for j in range(N * GC // 128):
            rows = pl.ds(group * N * GC + j * 128, 128)
            value = res_recv[rows, :] * gate_t[rows, :]
            gate_t[rows, :] = value
            total = total + jnp.sum((value * value).reshape(16, 8, 128), axis=0)
    total = jnp.broadcast_to(jnp.sum(total, axis=0, keepdims=True), (8, 128))
    sum_send[...] = total
    copies = []
    for k in range(1, TP):
        copies.append(
            pltpu.make_async_remote_copy(
                sum_send,
                sum_recv.at[k],
                sum_send_sem.at[k],
                sum_recv_sem.at[k],
                device_id={"tp": (tp + k) % TP},
                device_id_type=MESH,
            )
        )
    for copy in copies:
        copy.start()
    for j in range(8):
        lanes = pl.ds(j * 128, 128)
        gated[:, lanes] = gate_t[pl.ds(j * 128, 128), :].T * gain_ref[:, lanes]
    for k, copy in enumerate(copies):
        copy.wait()
        total = total + sum_recv[k + 1]
    scale = lax.rsqrt(total / (CHAN * TP) + EPS)
    scale = jnp.broadcast_to(scale[:1], (128, 128)).T
    for j in range(8):
        lanes = pl.ds(j * 128, 128)
        out_ref[:, lanes] = (gated[:, lanes] * scale).astype(BF16)

    landed(sig_send, 2 * (NEAR - 1) * SET, sig_send_sem)
    for copy in passes:
        copy.wait_send()
    for group in range(GROUPS):
        landed(fil_send, 2 * (NEAR - 1) * 4 * GC, fil_send_sem.at[group])
        for copy in far_copies(group):
            copy.wait_send()
        landed(res_send, 2 * (NEAR - 1) * GC, res_send_sem.at[group])


def local(gate_branch, key_branch, value_branch, spectrum_real, spectrum_imag, norm_gain):
    def lines(spectrum):
        split = spectrum.reshape(TOK, 2, CHAN // 128, 128)
        return split.transpose(0, 2, 1, 3).reshape(TOK * 2 * CHAN // 128, 128)

    args = (
        gate_branch,
        key_branch,
        value_branch,
        lines(spectrum_real),
        lines(spectrum_imag),
        norm_gain.reshape(1, CHAN),
    ) + tuple(jnp.asarray(table) for table in tables())
    vmem = pl.BlockSpec(memory_space=pltpu.VMEM)
    hbm = pl.BlockSpec(memory_space=pltpu.HBM)
    return pl.pallas_call(
        kernel,
        out_shape=jax.ShapeDtypeStruct((TOK, CHAN), BF16),
        in_specs=[hbm] * len(args),
        out_specs=vmem,
        scratch_shapes=[pltpu.VMEM(arg.shape[-2:], arg.dtype) for arg in args]
        + [
            pltpu.VMEM((CHAN, 128), F32),
            pltpu.VMEM((2 * CHAN, 128), F32),
            pltpu.VMEM((4 * CHAN, 128), F32),
            pltpu.VMEM((4 * CHAN, 128), F32),
            pltpu.VMEM((2 * SET * N, 256), F32),
            pltpu.VMEM((SET * N, 768), BF16),
            pltpu.VMEM((3 * N, SET * 128), BF16),
            pltpu.VMEM((6 * N, 2 * GC * 128), BF16),
            pltpu.VMEM((CHAN, 128), F32),
            pltpu.VMEM((CHAN, 128), F32),
            pltpu.VMEM((CHAN, 128), F32),
            pltpu.VMEM((CHAN, 128), F32),
            pltpu.VMEM((CHAN, 128), F32),
            pltpu.VMEM((TOK, CHAN), F32),
            pltpu.VMEM((8, 128), F32),
            pltpu.VMEM((TP, 8, 128), F32),
            pltpu.SemaphoreType.DMA,
            pltpu.SemaphoreType.DMA,
            pltpu.SemaphoreType.DMA((2,)),
            pltpu.SemaphoreType.DMA((2,)),
            pltpu.SemaphoreType.DMA((GROUPS,)),
            pltpu.SemaphoreType.DMA((GROUPS,)),
            pltpu.SemaphoreType.DMA((2 * GROUPS,)),
            pltpu.SemaphoreType.DMA((2 * GROUPS,)),
            pltpu.SemaphoreType.DMA((GROUPS,)),
            pltpu.SemaphoreType.DMA((GROUPS,)),
            pltpu.SemaphoreType.DMA((TP,)),
            pltpu.SemaphoreType.DMA((TP,)),
            pltpu.SemaphoreType.DMA((2 + 2 * GROUPS,)),
            pltpu.SemaphoreType.DMA((len(args),)),
        ],
        compiler_params=pltpu.CompilerParams(
            collective_id=0, has_side_effects=True, vmem_limit_bytes=62 << 20
        ),
    )(*args)


def solution(mesh):
    in_specs = (
        P("ctx", "tp"),
        P("ctx", "tp"),
        P("ctx", "tp"),
        P(None, "ctx", "tp"),
        P(None, "ctx", "tp"),
        P("tp"),
    )
    return jax.shard_map(
        local, mesh=mesh, in_specs=in_specs, out_specs=P("ctx", "tp"), check_vma=False
    )
```

```python
import functools

import jax
import jax.numpy as jnp
import ml_dtypes
import numpy as np
from jax import lax
from jax.experimental import pallas as pl
from jax.experimental.pallas import tpu as pltpu
from jax.sharding import PartitionSpec as P

MESH = pl.DeviceIdType.MESH
F32 = jnp.float32
BF16 = jnp.bfloat16
N = 64
TP = 4
TOK = 128
CHAN = 1024
FFT = 2 * N * TOK
EPS = 1e-05
NY, NZ = 4, 8
NEAR = N // 2
SET = CHAN // N
GC = 4
GROUPS = SET // GC
GROUP_TILES = N * GC // 128
MORE = 4
AHEAD = 2
LAG = 2


def split_table(table):
    high = table.astype(ml_dtypes.bfloat16)
    low = (table - high.astype(np.float64)).astype(ml_dtypes.bfloat16)
    return high, low


def tables():
    bits = N.bit_length() - 1
    place = np.arange(N)
    rev = np.zeros_like(place)
    for bit in range(bits):
        rev |= (place >> bit & 1) << (bits - 1 - bit)
    pos = np.arange(TOK)
    step, y, core = np.meshgrid(np.arange(4), np.arange(NY), np.arange(2), indexing="ij")

    def devices(plane):
        return ((y * NZ + plane % NZ) * 2 + core).reshape(-1)

    first, last, cos_turn, sin_turn = [], [], [], []
    for z in range(NZ):
        for near, far in (
            (devices(z - step), devices(z + 1 + step)),
            (devices(z + step), devices(z - 1 - step)),
        ):
            block = np.concatenate([near, far])
            residue = np.concatenate([2 * rev[near], 2 * rev[near] + 1])
            angle = 2 * np.pi / (2 * N) * ((residue[:, None] * block[None, :]) % (2 * N))
            table = np.concatenate([np.cos(angle), -np.sin(angle)])
            high, low = split_table(table)
            first.append(np.concatenate([high, high, low], axis=1))
            high, low = split_table(table.T / FFT)
            last.append(np.concatenate([high, high, low], axis=1))
            turn = 2 * np.pi / FFT * ((residue[:, None] * pos[None, :]) % FFT)
            cos_turn.append(np.cos(turn).astype(np.float32))
            sin_turn.append(np.sin(turn).astype(np.float32))

    def by_plane(pieces):
        return np.stack(pieces).reshape(NZ, -1, pieces[0].shape[1])

    inner = 2 * np.pi / TOK * ((pos[:, None] * pos[None, :]) % TOK)
    cos, sin = np.cos(inner), np.sin(inner)
    forward = np.block([[cos, -sin], [sin, cos]])
    high, low = split_table(forward)
    forward_cat = np.concatenate([high, high, low], axis=0)
    backward = np.block([[cos, sin], [-sin, cos]])
    high, low = split_table(backward)
    backward_cat = np.concatenate([high, high, low], axis=0)
    return (
        by_plane(first),
        forward_cat,
        backward_cat,
        by_plane(last),
        by_plane(cos_turn),
        by_plane(sin_turn),
    )


def parts(value):
    high = value.astype(BF16)
    return high, (value - high.astype(F32)).astype(BF16)


def device(y, z, core):
    return (y % NY * NZ + (z + NZ) % NZ) * 2 + core % 2


def kernel(
    gate_hbm,
    key_hbm,
    value_hbm,
    real_hbm,
    imag_hbm,
    gain_hbm,
    first_hbm,
    forward_hbm,
    backward_hbm,
    last_hbm,
    cos_hbm,
    sin_hbm,
    out_ref,
    gate_ref,
    key_ref,
    value_ref,
    real_ref,
    imag_ref,
    gain_ref,
    first_ref,
    forward_ref,
    backward_ref,
    last_ref,
    cos_ref,
    sin_ref,
    sig_send,
    sig_recv,
    fil_send,
    fil_recv,
    freq,
    rows_wide,
    cols_sig,
    cols_wide,
    far_send,
    far_recv,
    res_send,
    res_recv,
    gate_t,
    gated,
    mixed,
    sum_send,
    sum_recv,
    sig_send_sem,
    sig_recv_sem,
    pass_send_sem,
    pass_recv_sem,
    fil_send_sem,
    fil_recv_sem,
    far_send_sem,
    far_recv_sem,
    res_send_sem,
    res_recv_sem,
    sum_send_sem,
    sum_recv_sem,
    own_sem,
    load_sem,
):
    me = lax.axis_index("ctx")
    tp = lax.axis_index("tp")
    y, z, core = me // (2 * NZ), me // 2 % NZ, me % 2
    up, down = device(y, z + 1, core), device(y, z - 1, core)
    barrier = pltpu.get_barrier_semaphore()

    def greet(k, carry):
        step = k % 7
        step = (step + 1) // 2 * (2 * (step % 2) - 1)
        peer = device(y + k // 7 % NY, z + step, core + k // 28)
        pl.semaphore_signal(barrier, inc=1, device_id={"ctx": peer}, device_id_type=MESH)
        return carry

    lax.fori_loop(1, 56, greet, 0)
    for k in range(1, TP):
        pl.semaphore_signal(
            barrier, inc=1, device_id={"tp": (tp + k) % TP}, device_id_type=MESH
        )

    pairs = (
        (key_hbm, key_ref),
        (value_hbm, value_ref),
        (real_hbm, real_ref),
        (imag_hbm, imag_ref),
        (first_hbm.at[z], first_ref),
        (cos_hbm.at[z], cos_ref),
        (sin_hbm.at[z], sin_ref),
        (forward_hbm, forward_ref),
        (gate_hbm, gate_ref),
        (backward_hbm, backward_ref),
        (last_hbm.at[z], last_ref),
        (gain_hbm, gain_ref),
    )
    loads = [
        pltpu.make_async_copy(src, dst, load_sem.at[i]) for i, (src, dst) in enumerate(pairs)
    ]
    for load in loads:
        load.start()

    loads[0].wait()
    loads[1].wait()
    for j in range(8):
        lanes = pl.ds(j * 128, 128)
        turned = (key_ref[:, lanes].astype(F32) * value_ref[:, lanes].astype(F32)).T
        for i in range(128 // GC):
            group, chan_set = divmod((j * 128) // GC + i, N)
            sig_send[pl.ds(chan_set * SET + group * GC, GC), :] = turned[i * GC : i * GC + GC]

    pl.semaphore_wait(barrier, 55 + TP - 1)

    def reach(m):
        step = (m % 4 + m // 4) % 4
        return y + m % 4, core + m // 16, step, step * 8 + y * 2 + core

    def send_signal(m, carry):
        to_y, to_core, step, slot = reach(m)
        for side in range(2):
            plane = z + step if side == 0 else z - step
            chan_set = device(to_y, plane - side, to_core)
            pltpu.make_async_remote_copy(
                sig_send.at[pl.ds(chan_set * SET, SET)],
                sig_recv.at[pl.ds((side * N + slot) * SET, SET)],
                sig_send_sem,
                sig_recv_sem,
                device_id={"ctx": device(to_y, plane, to_core)},
                device_id_type=MESH,
            ).start()
        return carry

    lax.fori_loop(1, NEAR, send_signal, 0)

    def turn_filter(group):
        for j in range(group * GROUP_TILES, (group + 1) * GROUP_TILES):
            for e in range(2):
                for part, ref in enumerate((real_ref, imag_ref)):
                    turned = ref[pl.ds(j * 2 + e, 128, stride=16), :].T
                    for i in range(128 // GC):
                        row = (((j * 128) // GC + i) * 4 + e * 2 + part) * GC
                        fil_send[pl.ds(row, GC), :] = turned[i * GC : i * GC + GC]

    def send_filter(group):
        def send(m, carry):
            to_y, to_core, step, slot = reach(m)
            for side in range(2):
                plane = z + step if side == 0 else z - step
                chan_set = device(to_y, plane - side, to_core)
                pltpu.make_async_remote_copy(
                    fil_send.at[pl.ds((group * N + chan_set) * 4 * GC, 4 * GC)],
                    fil_recv.at[pl.ds(((group * 2 + side) * NEAR + slot) * 4 * GC, 4 * GC)],
                    fil_send_sem.at[group],
                    fil_recv_sem.at[group],
                    device_id={"ctx": device(to_y, plane, to_core)},
                    device_id_type=MESH,
                ).start()
            return carry

        lax.fori_loop(1, NEAR, send, 0)

    loads[2].wait()
    loads[3].wait()
    for group in range(GROUPS):
        turn_filter(group)
        if group < AHEAD:
            send_filter(group)

    sets = (me, down)
    own_slot = y * 2 + core
    own_signal, own_filter = [], []
    for side in range(2):
        own_signal.append(
            pltpu.make_async_copy(
                sig_send.at[pl.ds(sets[side] * SET, SET)],
                sig_recv.at[pl.ds((side * N + own_slot) * SET, SET)],
                own_sem.at[side],
            )
        )
        for group in range(GROUPS):
            own_filter.append(
                pltpu.make_async_copy(
                    fil_send.at[pl.ds((group * N + sets[side]) * 4 * GC, 4 * GC)],
                    fil_recv.at[pl.ds(((group * 2 + side) * NEAR + own_slot) * 4 * GC, 4 * GC)],
                    own_sem.at[2 + side * GROUPS + group],
                )
            )
    for copy in own_signal + own_filter:
        copy.start()

    for load in loads[4:]:
        load.wait()
    for j in range(8):
        gate_t[pl.ds(j * 128, 128), :] = gate_ref[:, pl.ds(j * 128, 128)].astype(F32).T

    def landed(buffer, rows, sem):
        view = buffer.at[pl.ds(0, rows)]
        pltpu.make_async_copy(view, view, sem).wait()

    for copy in own_signal:
        copy.wait()
    landed(sig_recv, 2 * (NEAR - 1) * SET, sig_recv_sem)
    passes = [
        pltpu.make_async_remote_copy(
            sig_recv.at[pl.ds(side * N * SET, NEAR * SET)],
            sig_recv.at[pl.ds(((1 - side) * N + NEAR) * SET, NEAR * SET)],
            pass_send_sem.at[side],
            pass_recv_sem.at[1 - side],
            device_id={"ctx": (up, down)[side]},
            device_id_type=MESH,
        )
        for side in range(2)
    ]
    for copy in passes:
        copy.start()
    for group in range(AHEAD, MORE):
        send_filter(group)
    for side in range(2):
        far = sig_recv.at[pl.ds((side * N + NEAR) * SET, NEAR * SET)]
        pltpu.make_async_copy(far, far, pass_recv_sem.at[side]).wait()

    for side in range(2):
        for c in range(SET):
            high, low = parts(sig_recv[pl.ds(side * N * SET + c, N, stride=SET), :])
            lanes = pl.ds(c * 128, 128)
            cols_sig[pl.ds(0, N), lanes] = high
            cols_sig[pl.ds(N, N), lanes] = low
            cols_sig[pl.ds(2 * N, N), lanes] = high
        cos, sin = cos_ref[pl.ds(side * N, N), :], sin_ref[pl.ds(side * N, N), :]
        for pair in range(SET // 2):
            mid = jnp.dot(
                first_ref[pl.ds(side * 128, 128), :],
                cols_sig[:, pl.ds(pair * 256, 256)],
                preferred_element_type=F32,
            )
            for i in range(2):
                re, im = mid[:N, i * 128 : i * 128 + 128], mid[N:, i * 128 : i * 128 + 128]
                rows = pl.ds((pair * 2 + i) * N, N)
                high, low = parts(re * cos + im * sin)
                rows_wide[rows, pl.ds(0, 128)] = high
                rows_wide[rows, pl.ds(256, 128)] = low
                rows_wide[rows, pl.ds(512, 128)] = high
                high, low = parts(im * cos - re * sin)
                rows_wide[rows, pl.ds(128, 128)] = high
                rows_wide[rows, pl.ds(384, 128)] = low
                rows_wide[rows, pl.ds(640, 128)] = high
        for quad in range(SET // 4):
            freq[pl.ds((side * SET + quad * 4) * N, 4 * N), :] = jnp.dot(
                rows_wide[pl.ds(quad * 4 * N, 4 * N), :],
                forward_ref[...],
                preferred_element_type=F32,
            )

    far_rows = NEAR * GC

    def inverse(group):
        for side in range(2):
            own_filter[side * GROUPS + group].wait()
        landed(fil_recv, 2 * (NEAR - 1) * 4 * GC, fil_recv_sem.at[group])
        for side in range(2):
            for c in range(GC):
                for e in range(2):
                    base = (group * 2 + side) * NEAR * 4 * GC + e * 2 * GC + c
                    f_re = fil_recv[pl.ds(base, NEAR, stride=4 * GC), :]
                    f_im = fil_recv[pl.ds(base + GC, NEAR, stride=4 * GC), :]
                    src = pl.ds((side * SET + group * GC + c) * N + e * NEAR, NEAR)
                    x_re = freq[src, pl.ds(0, 128)]
                    x_im = freq[src, pl.ds(128, 128)]
                    rows = pl.ds((side * GC + c) * N + e * NEAR, NEAR)
                    high, low = parts(x_re * f_re - x_im * f_im)
                    rows_wide[rows, pl.ds(0, 128)] = high
                    rows_wide[rows, pl.ds(256, 128)] = low
                    rows_wide[rows, pl.ds(512, 128)] = high
                    high, low = parts(x_re * f_im + x_im * f_re)
                    rows_wide[rows, pl.ds(128, 128)] = high
                    rows_wide[rows, pl.ds(384, 128)] = low
                    rows_wide[rows, pl.ds(640, 128)] = high
        for quad in range(2 * GC // 4):
            back = jnp.dot(
                rows_wide[pl.ds(quad * 4 * N, 4 * N), :],
                backward_ref[...],
                preferred_element_type=F32,
            )
            for i in range(4):
                side, c = divmod(quad * 4 + i, GC)
                lanes = pl.ds((side * GC + c) * 128, 128)
                cos, sin = cos_ref[pl.ds(side * N, N), :], sin_ref[pl.ds(side * N, N), :]
                re, im = back[i * N : i * N + N, :128], back[i * N : i * N + N, 128:]
                high, low = parts(re * cos - im * sin)
                cols_wide[pl.ds(0, N), lanes] = high
                cols_wide[pl.ds(2 * N, N), lanes] = low
                cols_wide[pl.ds(4 * N, N), lanes] = high
                high, low = parts(re * sin + im * cos)
                cols_wide[pl.ds(N, N), lanes] = high
                cols_wide[pl.ds(3 * N, N), lanes] = low
                cols_wide[pl.ds(5 * N, N), lanes] = high
        for side in range(2):
            for pair in range(GC // 2):
                conv = jnp.dot(
                    last_ref[pl.ds(side * N, N), :],
                    cols_wide[:, pl.ds((side * GC + pair * 2) * 128, 256)],
                    preferred_element_type=F32,
                )
                for i in range(2):
                    base = (group * 2 + side) * far_rows + pair * 2 + i
                    rows = pl.ds(base, NEAR, stride=GC)
                    res_send[rows, :] = conv[:NEAR, i * 128 : i * 128 + 128]
                    far_send[rows, :] = conv[NEAR:, i * 128 : i * 128 + 128]

    def far_copies(group):
        return [
            pltpu.make_async_remote_copy(
                far_send.at[pl.ds((group * 2 + side) * far_rows, far_rows)],
                far_recv.at[pl.ds((group * 2 + 1 - side) * far_rows, far_rows)],
                far_send_sem.at[group * 2 + side],
                far_recv_sem.at[group * 2 + 1 - side],
                device_id={"ctx": (up, down)[side]},
                device_id_type=MESH,
            )
            for side in range(2)
        ]

    own_result = []

    def finish(group):
        for side in range(2):
            rows = pl.ds((group * 2 + side) * far_rows, far_rows)
            view = far_recv.at[rows]
            pltpu.make_async_copy(view, view, far_recv_sem.at[group * 2 + side]).wait()
            res_send[rows, :] = res_send[rows, :] + far_recv[rows, :]

        def send(m, carry):
            step = (m % 4 + m // 4) % 4
            to_y, to_core = (y + m % 4) % NY, (core + m // 16) % 2
            slot = step * 8 + to_y * 2 + to_core
            for side in range(2):
                plane = z - step if side == 0 else z + step
                pltpu.make_async_remote_copy(
                    res_send.at[pl.ds(((group * 2 + side) * NEAR + slot) * GC, GC)],
                    res_recv.at[pl.ds((group * N + sets[side]) * GC, GC)],
                    res_send_sem.at[group],
                    res_recv_sem.at[group],
                    device_id={"ctx": device(to_y, plane, to_core)},
                    device_id_type=MESH,
                ).start()
            return carry

        lax.fori_loop(1, NEAR, send, 0, unroll=True)
        for side in range(2):
            copy = pltpu.make_async_copy(
                res_send.at[pl.ds(((group * 2 + side) * NEAR + own_slot) * GC, GC)],
                res_recv.at[pl.ds((group * N + sets[side]) * GC, GC)],
                own_sem.at[side],
            )
            copy.start()
            own_result.append(copy)

    for group in range(GROUPS):
        inverse(group)
        for copy in far_copies(group):
            copy.start()
        if group + MORE < GROUPS:
            send_filter(group + MORE)
        if group >= LAG:
            finish(group - LAG)
    for group in range(GROUPS - LAG, GROUPS):
        finish(group)

    for side in range(2):
        view = res_send.at[pl.ds(0, GROUPS * GC)]
        pltpu.make_async_copy(view, view, own_sem.at[side]).wait()
    total = jnp.zeros((8, 128), F32)
    for group in range(GROUPS):
        landed(res_recv, 2 * (NEAR - 1) * GC, res_recv_sem.at[group])
        for j in range(N * GC // 128):
            rows = pl.ds(group * N * GC + j * 128, 128)
            value = res_recv[rows, :] * gate_t[rows, :]
            gate_t[rows, :] = value
            total = total + jnp.sum((value * value).reshape(16, 8, 128), axis=0)
    total = jnp.broadcast_to(jnp.sum(total, axis=0, keepdims=True), (8, 128))
    sum_send[...] = total
    copies = []
    for k in range(1, TP):
        copies.append(
            pltpu.make_async_remote_copy(
                sum_send,
                sum_recv.at[k],
                sum_send_sem.at[k],
                sum_recv_sem.at[k],
                device_id={"tp": (tp + k) % TP},
                device_id_type=MESH,
            )
        )
    for copy in copies:
        copy.start()
    for j in range(8):
        lanes = pl.ds(j * 128, 128)
        gated[:, lanes] = gate_t[pl.ds(j * 128, 128), :].T * gain_ref[:, lanes]
    for k, copy in enumerate(copies):
        copy.wait()
        total = total + sum_recv[k + 1]
    scale = lax.rsqrt(total / (CHAN * TP) + EPS)
    scale = jnp.broadcast_to(scale[:1], (128, 128)).T
    stores = []
    for j in range(4):
        lanes = pl.ds(j * 256, 256)
        wide = jnp.concatenate([scale, scale], axis=1)
        mixed[:, lanes] = (gated[:, lanes] * wide).astype(BF16)
        stores.append(
            pltpu.make_async_copy(mixed.at[:, lanes], out_ref.at[:, lanes], load_sem.at[j])
        )
        stores[-1].start()

    for store in stores:
        store.wait()
    landed(sig_send, 2 * (NEAR - 1) * SET, sig_send_sem)
    for copy in passes:
        copy.wait_send()
    for group in range(GROUPS):
        landed(fil_send, 2 * (NEAR - 1) * 4 * GC, fil_send_sem.at[group])
        for copy in far_copies(group):
            copy.wait_send()
        landed(res_send, 2 * (NEAR - 1) * GC, res_send_sem.at[group])


def local(gate_branch, key_branch, value_branch, spectrum_real, spectrum_imag, norm_gain):
    def lines(spectrum):
        split = spectrum.reshape(TOK, 2, CHAN // 128, 128)
        return split.transpose(0, 2, 1, 3).reshape(TOK * 2 * CHAN // 128, 128)

    args = (
        gate_branch,
        key_branch,
        value_branch,
        lines(spectrum_real),
        lines(spectrum_imag),
        norm_gain.reshape(1, CHAN),
    ) + tuple(jnp.asarray(table) for table in tables())
    hbm = pl.BlockSpec(memory_space=pltpu.HBM)
    return pl.pallas_call(
        kernel,
        out_shape=jax.ShapeDtypeStruct((TOK, CHAN), BF16),
        in_specs=[hbm] * len(args),
        out_specs=hbm,
        scratch_shapes=[pltpu.VMEM(arg.shape[-2:], arg.dtype) for arg in args]
        + [
            pltpu.VMEM((CHAN, 128), F32),
            pltpu.VMEM((2 * CHAN, 128), F32),
            pltpu.VMEM((4 * CHAN, 128), F32),
            pltpu.VMEM((4 * CHAN, 128), F32),
            pltpu.VMEM((2 * SET * N, 256), F32),
            pltpu.VMEM((SET * N, 768), BF16),
            pltpu.VMEM((3 * N, SET * 128), BF16),
            pltpu.VMEM((6 * N, 2 * GC * 128), BF16),
            pltpu.VMEM((CHAN, 128), F32),
            pltpu.VMEM((CHAN, 128), F32),
            pltpu.VMEM((CHAN, 128), F32),
            pltpu.VMEM((CHAN, 128), F32),
            pltpu.VMEM((CHAN, 128), F32),
            pltpu.VMEM((TOK, CHAN), F32),
            pltpu.VMEM((TOK, CHAN), BF16),
            pltpu.VMEM((8, 128), F32),
            pltpu.VMEM((TP, 8, 128), F32),
            pltpu.SemaphoreType.DMA,
            pltpu.SemaphoreType.DMA,
            pltpu.SemaphoreType.DMA((2,)),
            pltpu.SemaphoreType.DMA((2,)),
            pltpu.SemaphoreType.DMA((GROUPS,)),
            pltpu.SemaphoreType.DMA((GROUPS,)),
            pltpu.SemaphoreType.DMA((2 * GROUPS,)),
            pltpu.SemaphoreType.DMA((2 * GROUPS,)),
            pltpu.SemaphoreType.DMA((GROUPS,)),
            pltpu.SemaphoreType.DMA((GROUPS,)),
            pltpu.SemaphoreType.DMA((TP,)),
            pltpu.SemaphoreType.DMA((TP,)),
            pltpu.SemaphoreType.DMA((2 + 2 * GROUPS,)),
            pltpu.SemaphoreType.DMA((len(args),)),
        ],
        compiler_params=pltpu.CompilerParams(
            collective_id=0, has_side_effects=True, vmem_limit_bytes=62 << 20
        ),
    )(*args)


def solution(mesh):
    in_specs = (
        P("ctx", "tp"),
        P("ctx", "tp"),
        P("ctx", "tp"),
        P(None, "ctx", "tp"),
        P(None, "ctx", "tp"),
        P("tp"),
    )
    return jax.shard_map(
        local, mesh=mesh, in_specs=in_specs, out_specs=P("ctx", "tp"), check_vma=False
    )
```
